256 devices in a mesh: zone: 64 (over z, y, core), band: 4 (over x).
Axes of the slice: x: 4, y: 4, z: 8, core: 2. Of those that a mesh axis runs over, the one named last changes fastest.
Arguments:
- pixels: float32 [32768, 32, 128], P(('zone', 'band')), may hold values from -6 to 6
- inv_var: float32 [32768, 32, 128], P(('zone', 'band')), may hold values from 0.25 to 4
- tile_offset: float32 [2, 32768], P(None, ('zone', 'band')), may hold values from 12 to 116, as said below
- psf_amp: float32 [3, 32768], P(None, ('zone', 'band')), may hold values from 0.3 to 1
- psf_sigma: float32 [3, 32768], P(None, ('zone', 'band')), may hold values from 0.9 to 2
- tile_blob: int32 [32768], P(('zone', 'band')), may hold values from 0 to 4095, as said below
- tile_band: int32 [32768], P(('zone', 'band')), may hold values from 0 to 2
- source_pos: float32 [2, 32768], P(None, 'zone'), may hold values from -5.3 to 5.3
- edge_rows: int32 [8192], P('zone'), may hold values from 0 to 511, as said below
- blob_members: int32 [4096, 16], P('zone'), may hold values from 0 to 639, as said below
- sources_per_blob: int32 [4096], P('zone'), may hold values from 1 to 16, as said below
Outputs:
- fluxes: float32 [3, 32768], P(None, 'zone')
The draws below stay inside these ranges and needn't reach their ends.
Inputs may be any that keep to these rules, and one draw needn't show every extreme that they name: `tile_blob`: blob b lies in zone b // 64. Of one device's 128 tiles at most 4 cover blobs of one zone, and in every draw some zone receives exactly 4 tiles from every device of each band group. `edge_rows`: per zone, 64 lower edge rows then 64 upper edge rows, local row numbers, all 128 distinct. `blob_members`: slots at or beyond the blob's count hold 0. Every source is the live member of exactly one blob: a zone's lower edge rows belong to blobs of the previous zone and its upper edge rows to blobs of the next zone, except the first zone's lower and the last zone's upper rows, which stay in their own zone; the first zone never names the first 64 entries, the last zone never the last 64. `sources_per_blob`: the counts of one zone sum to 512; in every zone some blob has 16. `tile_offset`: row offsets lie within 12 to 20.
All inputs are finite; a program needn't handle non-finite values.
Results may differ from the reference program's by a relative error of at most 0.0003.
Values sent between devices are 32-bit elements; how exact they have to be, the bound alone decides.
No kernel may reach another device: no remote copies, remote signals or barrier semaphores. Data moves between devices by JAX's collectives and lax.ppermute only.
A program may use at most 64 MiB of HBM per device.

```python
import math
import jax
import jax.numpy as jnp
from jax import lax

FILTER_BANDS = 3
COMPS = 3
MAX_SOURCES = 16
PH = 32
PW = 128
SRC_DEV = 512
TILE_DEV = 128
BLOB_DEV = 64
EDGE = 64
CAP = 4
TILES = 32768
N_ZONE = 64
N_BAND = 4


def layout(key):
    key = jax.random.fold_in(key, 31)
    key_edge, key_claim, key_full, key_cells = jax.random.split(key, 4)
    extent = SRC_DEV + 2 * EDGE
    zone_ids = jnp.arange(N_ZONE, dtype=jnp.int32)
    edge_lists = jax.vmap(lambda sub_key: jax.random.permutation(sub_key, SRC_DEV)[:2 * EDGE])(jax.random.split(key_edge, N_ZONE)).astype(jnp.int32)
    lower_rows = edge_lists[:, :EDGE]
    upper_rows = edge_lists[:, EDGE:]

    def one_zone(zone_id, lower_list, upper_list, claim_key, full_key, cells_key):
        own_flags = jnp.ones((SRC_DEV,), jnp.int32)
        own_flags = own_flags.at[lower_list].set(jnp.where(zone_id > 0, 0, 1))
        own_flags = own_flags.at[upper_list].set(jnp.where(zone_id < N_ZONE - 1, 0, 1))
        before_flags = jnp.full((EDGE,), jnp.where(zone_id > 0, 1, 0), jnp.int32)
        after_flags = jnp.full((EDGE,), jnp.where(zone_id < N_ZONE - 1, 1, 0), jnp.int32)
        claimed = jnp.concatenate([before_flags, own_flags, after_flags])
        shuffle = jax.random.permutation(claim_key, extent).astype(jnp.int32)
        ranking = jnp.where(claimed == 1, shuffle, shuffle + extent)
        claim_order = jnp.argsort(ranking).astype(jnp.int32)
        cell_total = BLOB_DEV * (MAX_SOURCES - 1)
        full_blob = jax.random.randint(full_key, (), 0, BLOB_DEV)
        cell_shuffle = jax.random.permutation(cells_key, cell_total).astype(jnp.int32)
        cell_blob = jnp.arange(cell_total, dtype=jnp.int32) // (MAX_SOURCES - 1)
        cell_score = jnp.where(cell_blob == full_blob, cell_shuffle - cell_total, cell_shuffle)
        cell_rank = jnp.argsort(jnp.argsort(cell_score)).astype(jnp.int32)
        chosen = (cell_rank < SRC_DEV - BLOB_DEV).astype(jnp.int32)
        counts = 1 + jnp.sum(chosen.reshape(BLOB_DEV, MAX_SOURCES - 1), axis=1)
        starts = jnp.cumsum(counts) - counts
        slot_ids = jnp.arange(MAX_SOURCES, dtype=jnp.int32)
        live_slots = slot_ids[None, :] < counts[:, None]
        picks = jnp.clip(starts[:, None] + slot_ids[None, :], 0, SRC_DEV - 1)
        members = jnp.where(live_slots, claim_order[picks], 0).astype(jnp.int32)
        slot_table = jnp.broadcast_to(slot_ids[None, :], members.shape)
        slot_of = jnp.zeros((extent,), jnp.int32).at[jnp.where(live_slots, members, extent)].set(slot_table, mode='drop')
        return (members, counts.astype(jnp.int32), slot_of)
    members, counts, slot_of = jax.vmap(one_zone)(zone_ids, lower_rows, upper_rows, jax.random.split(key_claim, N_ZONE), jax.random.split(key_full, N_ZONE), jax.random.split(key_cells, N_ZONE))
    own_slots = slot_of[:, EDGE:EDGE + SRC_DEV]
    next_parts = slot_of[:, EDGE + SRC_DEV:]
    prev_parts = slot_of[:, :EDGE]
    lower_values = jnp.concatenate([next_parts[:1], next_parts[:-1]], axis=0)
    upper_values = jnp.concatenate([prev_parts[1:], prev_parts[-1:]], axis=0)

    def place(slots, lower_list, upper_list, lower_vals, upper_vals, zone_id):
        slots = slots.at[lower_list].set(jnp.where(zone_id > 0, lower_vals, slots[lower_list]))
        slots = slots.at[upper_list].set(jnp.where(zone_id < N_ZONE - 1, upper_vals, slots[upper_list]))
        return slots
    source_slots = jax.vmap(place)(own_slots, lower_rows, upper_rows, lower_values, upper_values, zone_ids)
    return (edge_lists, members, counts, source_slots)


def draw_edge_rows(key, part):
    return layout(key)[0].reshape(-1)


def draw_blob_members(key, part):
    return layout(key)[1].reshape(-1, MAX_SOURCES)


def draw_sources_per_blob(key, part):
    return layout(key)[2].reshape(-1)


def draw_source_pos(key, part):
    source_slots = layout(key)[3]
    jitter_key = jax.random.fold_in(key, 57)
    jitter_reach = 0.5
    jitter_noise = jax.random.uniform(jitter_key, (2, N_ZONE * SRC_DEV), jnp.float32, -jitter_reach, jitter_reach)
    flat_slots = source_slots.reshape(-1)
    lattice_row = (flat_slots // 4).astype(jnp.float32) * 3.0 - 4.5
    lattice_col = (flat_slots % 4).astype(jnp.float32) * 3.0 - 4.5
    return jnp.stack([lattice_row, lattice_col]) + jitter_noise


def draw_tile_offset(key, part):
    key = jax.random.fold_in(key, 97)
    row_key, col_key = jax.random.split(key)
    offset_rows = jax.random.uniform(row_key, (TILES,), jnp.float32, 12.0, 20.0)
    offset_cols = jax.random.uniform(col_key, (TILES,), jnp.float32, 12.0, PW - 12.0)
    return jnp.stack([offset_rows, offset_cols])


def draw_tile_blob(key, part):
    key = jax.random.fold_in(key, 83)
    key_busy, key_slots, key_order, key_local = jax.random.split(key, 4)
    holders = N_ZONE * N_BAND
    busy_zone = jax.random.randint(key_busy, (), 0, N_ZONE)
    free_slots = (N_ZONE - 1) * CAP
    picked = jax.vmap(lambda sub_key: jax.random.permutation(sub_key, free_slots)[:TILE_DEV - CAP])(jax.random.split(key_slots, holders))
    other_zone = (busy_zone + 1 + picked // CAP) % N_ZONE
    zone_list = jnp.concatenate([jnp.full((holders, CAP), busy_zone, jnp.int32), other_zone.astype(jnp.int32)], axis=1)
    order_perm = jax.vmap(lambda sub_key: jax.random.permutation(sub_key, TILE_DEV))(jax.random.split(key_order, holders))
    zone_list = jnp.take_along_axis(zone_list, order_perm, axis=1)
    local_blob = jax.random.randint(key_local, (holders, TILE_DEV), 0, BLOB_DEV)
    return (zone_list * BLOB_DEV + local_blob).reshape(-1).astype(jnp.int32)


def place_ends(drawn, stream_key, least, high):
    shape = drawn.shape
    spot = [jax.random.randint(jax.random.fold_in(stream_key, axis), (), 0, shape[axis]) for axis in range(len(shape))]
    drawn = drawn.at[tuple(spot)].set(least)
    longest = shape.index(max(shape))
    spot[longest] = (spot[longest] + 1) % shape[longest]
    return drawn.at[tuple(spot)].set(high)


def block_levels(key, shape, shards, smallest, largest):
    level = 1.0
    for dim, parts in shards:
        draws = jax.random.uniform(jax.random.fold_in(jax.random.fold_in(key, 6), dim), (parts,), jnp.float32, smallest / len(shards), largest / len(shards))
        level = level * jnp.repeat(jnp.exp(draws), shape[dim] // parts).reshape((-1,) + (1,) * (len(shape) - 1 - dim))
    return level


def centred(rng, shape, scale, bound, pieces=(), kind=jnp.bfloat16):
    drawn = scale * jax.random.normal(rng, shape, jnp.float32)
    if pieces:
        drawn = drawn * block_levels(rng, shape, pieces, -0.22, 0.18)
    return jnp.clip(drawn, -bound, bound).astype(kind)


def setup_inputs(seed: int = 0) -> dict:
    seeds = jax.random.split(jax.random.key(seed), 12)
    return {
        "pixels": centred(seeds[0], (TILES, PH, PW), 1.0, 6.0, ((0, 256),), jnp.float32),
        "inv_var": jnp.clip(jnp.exp(math.log(4.0) - 2.7725887 * jax.random.uniform(seeds[1], (TILES, PH, PW), jnp.float32) ** block_levels(seeds[1], (TILES, PH, PW), ((0, 256),), -0.2, 0.2)), 0.25, 4.0),
        "tile_offset": draw_tile_offset(jax.random.fold_in(seeds[11], 71), 0),
        "psf_amp": jnp.clip(jnp.exp(math.log(1.0) - 1.2039728 * jax.random.uniform(seeds[3], (COMPS, TILES), jnp.float32) ** block_levels(seeds[3], (COMPS, TILES), ((1, 256),), -0.2, 0.2)), 0.3, 1.0),
        "psf_sigma": jnp.clip(jnp.exp(math.log(2.0) - 0.798507723 * jax.random.uniform(seeds[4], (COMPS, TILES), jnp.float32) ** block_levels(seeds[4], (COMPS, TILES), ((1, 256),), -0.2, 0.2)), 0.9, 2.0),
        "tile_blob": draw_tile_blob(jax.random.fold_in(seeds[11], 71), 0),
        "tile_band": place_ends(jax.random.randint(seeds[6], (TILES,), 0, FILTER_BANDS), jax.random.fold_in(seeds[6], 1), 0, FILTER_BANDS - 1).astype(jnp.int32),
        "source_pos": draw_source_pos(jax.random.fold_in(seeds[11], 71), 0),
        "edge_rows": draw_edge_rows(jax.random.fold_in(seeds[11], 71), 0),
        "blob_members": draw_blob_members(jax.random.fold_in(seeds[11], 71), 0),
        "sources_per_blob": draw_sources_per_blob(jax.random.fold_in(seeds[11], 71), 0),
    }


HIGH = lax.Precision.HIGHEST
PRIOR = 1.0

def terms_per_tile(tile_image_pixels, tile_weight_pixels, pixel_shift, source_amplitude, profile_widths, source_location, slot_alive_flags):
    pixel_rows = jnp.arange(tile_image_pixels.shape[0]).astype(jnp.float32)
    pixel_cols = jnp.arange(tile_image_pixels.shape[1]).astype(jnp.float32)
    inverse_spread = 0.5 / (profile_widths * profile_widths)
    row_displacement = pixel_rows[None, :] - pixel_shift[0] - source_location[0][:, None]
    delta_col = pixel_cols[None, :] - pixel_shift[1] - source_location[1][:, None]
    row_profile = jnp.exp(-inverse_spread[None, :, None] * (row_displacement * row_displacement)[:, None, :]) * (source_amplitude[None, :, None] * slot_alive_flags[:, None, None])
    profile_col = jnp.exp(-inverse_spread[None, :, None] * (delta_col * delta_col)[:, None, :])
    rendered = jnp.sum(row_profile[:, :, :, None] * profile_col[:, :, None, :], axis=1).reshape(row_profile.shape[0], -1)
    weighted = rendered * tile_weight_pixels.reshape(1, -1)
    normal = jnp.einsum('sp,tp->st', weighted, rendered, precision=HIGH)
    projected = jnp.einsum('sp,p->s', weighted, tile_image_pixels.reshape(-1), precision=HIGH)
    return (normal, projected)

def reference(pixels, inv_var, tile_offset, psf_amp, psf_sigma, tile_blob, tile_band, source_pos, edge_rows, blob_members, sources_per_blob):
    blob_total = BLOB_DEV * N_ZONE
    edges = edge_rows.reshape(N_ZONE, 2, EDGE)
    zone_of = (jnp.arange(blob_total, dtype=jnp.int32) // BLOB_DEV)[:, None]
    before_zone = jnp.clip(zone_of - 1, 0, N_ZONE - 1)
    after_zone = jnp.clip(zone_of + 1, 0, N_ZONE - 1)
    from_prev = edges[before_zone, 1, jnp.clip(blob_members, 0, EDGE - 1)] + before_zone * SRC_DEV
    from_own = zone_of * SRC_DEV + jnp.clip(blob_members - EDGE, 0, SRC_DEV - 1)
    from_next = edges[after_zone, 0, jnp.clip(blob_members - EDGE - SRC_DEV, 0, EDGE - 1)] + after_zone * SRC_DEV
    source_of = jnp.where(blob_members < EDGE, from_prev, jnp.where(blob_members < EDGE + SRC_DEV, from_own, from_next)).astype(jnp.int32)
    alive = (jnp.arange(MAX_SOURCES, dtype=jnp.int32)[None, :] < sources_per_blob[:, None]).astype(jnp.float32)
    member_pos = jnp.transpose(source_pos[:, source_of], (1, 0, 2))
    tile_pos = member_pos[tile_blob]
    tile_alive = alive[tile_blob]

    def single_tile(packed):
        return terms_per_tile(*packed)
    normal, projected = lax.map(single_tile, (pixels, inv_var, tile_offset.T, psf_amp.T, psf_sigma.T, tile_pos, tile_alive), batch_size=16)
    target = (tile_blob * FILTER_BANDS + tile_band).astype(jnp.int32)
    normal_total = jax.ops.segment_sum(normal, target, num_segments=blob_total * FILTER_BANDS)
    rhs_total = jax.ops.segment_sum(projected, target, num_segments=blob_total * FILTER_BANDS)
    system = normal_total + PRIOR * jnp.eye(MAX_SOURCES, dtype=jnp.float32)[None, :, :]
    solved_fluxes = jnp.linalg.solve(system, rhs_total[:, :, None])[:, :, 0]
    value_entries = solved_fluxes.reshape(blob_total, FILTER_BANDS, MAX_SOURCES) * alive[:, None, :]
    spread = jnp.transpose(value_entries, (1, 0, 2)).reshape(FILTER_BANDS, -1)
    fluxes = jnp.zeros((FILTER_BANDS, SRC_DEV * N_ZONE), jnp.float32).at[:, source_of.reshape(-1)].add(spread)
    return fluxes
```

```python
import functools

import jax
import jax.numpy as jnp
from jax import lax
from jax.experimental import pallas as pl
from jax.experimental.pallas import tpu as pltpu
from jax.sharding import PartitionSpec as P

BANDS = 3
SLOTS = 16
PH = 32
PW = 128
SRC = 512
BLOBS = 64
EDGE = 64
GROUP = 8
TABLE_ROWS = 16
MARK = 1000.0
LOG2E = 1.4426950408889634
F32 = jnp.float32
BF16 = jnp.bfloat16
NT = (((1,), (1,)), ((), ()))
NN = (((1,), (0,)), ((), ()))
TN = (((0,), (0,)), ((), ()))
VMEM = pl.BlockSpec(memory_space=pltpu.VMEM)
SMEM = pl.BlockSpec(memory_space=pltpu.SMEM)


def iota(shape, axis):
    return lax.broadcasted_iota(jnp.int32, shape, axis)


def three_parts(x):
    high = x.astype(BF16)
    rest = x - high.astype(F32)
    mid = rest.astype(BF16)
    low = (rest - mid.astype(F32)).astype(BF16)
    return high, mid, low


def dot(a, b, dims):
    return lax.dot_general(a, b, dims, preferred_element_type=F32)


def exact_left(x, onehot, dims):
    high, mid, low = three_parts(x)
    return (dot(low, onehot, dims) + dot(mid, onehot, dims)) + dot(high, onehot, dims)


def table_kernel(members, counts, source_pos, edge_rows, out):
    cnt = counts[...]
    above = iota((BLOBS, BLOBS), 0)
    beside = iota((BLOBS, BLOBS), 1)
    spread = jnp.broadcast_to(cnt, (BLOBS, BLOBS))
    start = jnp.sum(jnp.where(beside < above, spread, 0.0), axis=1, keepdims=True)
    own = jnp.sum(jnp.where(beside == above, spread, 0.0), axis=1, keepdims=True)
    start_row = jnp.sum(jnp.where(above == beside, start, 0.0), axis=0, keepdims=True)
    entry = iota((BLOBS, SRC), 1).astype(F32)
    inside = jnp.logical_and(entry >= start, entry < start + own)
    slot = jnp.sum(jnp.where(inside, entry - start, 0.0), axis=0, keepdims=True)
    picked = exact_left(members[...].astype(F32), inside.astype(BF16), TN)
    slot_ids = iota((SLOTS, SRC), 0).astype(F32)
    source = jnp.sum(jnp.where(slot_ids == slot, picked, 0.0), axis=0, keepdims=True)
    wanted = jnp.concatenate([source, edge_rows[...].astype(F32) + float(EDGE)], axis=1)
    width = SRC + 2 * EDGE
    row_ids = iota((SRC, width), 0).astype(F32) + float(EDGE)
    onehot = jnp.where(row_ids == wanted, 1.0, 0.0).astype(BF16)
    pos = jnp.concatenate([source_pos[...], jnp.zeros((6, SRC), F32)], axis=0)
    got = exact_left(pos, onehot, NN)
    lanes = iota((1, width), 1)
    mark = jnp.where(wanted < float(EDGE), wanted + (MARK + EDGE), wanted + (MARK - EDGE - SRC))
    outside = jnp.logical_or(wanted < float(EDGE), wanted >= float(EDGE + SRC))
    marked = jnp.logical_and(lanes < SRC, outside)
    got = jnp.where(marked, mark, got)
    rows = [got[p : p + 1, PW * n : PW * (n + 1)] for p in range(2) for n in range(4)]
    rows += [got[p : p + 1, SRC : SRC + PW] for p in range(2)]
    rows.append(jnp.concatenate([start_row, cnt], axis=1))
    rows.append(jnp.zeros((TABLE_ROWS - 11, PW), F32))
    table = jnp.concatenate(rows, axis=0)

    def write(z, _):
        out[z] = table
        return 0

    lax.fori_loop(0, out.shape[0], write, 0, unroll=8)


def tile_kernel(
    blob_s,
    band_s,
    off_s,
    amp_s,
    inv_s,
    table,
    pixels,
    weights,
    out,
    buf_a,
    buf_b,
    roots,
    full,
    info,
    ranges,
    used,
):
    zones = table.shape[0]
    tiles = pixels.shape[0] // PH
    lane = iota((8, PW), 1)
    sub = iota((8, PW), 0)
    lane16 = iota((SLOTS, PW), 1).astype(F32)
    slot_f = iota((SLOTS, PW), 0).astype(F32)
    spot = lane >> 4
    entry = lane & (SLOTS - 1)

    def clear(z, _):
        out[z] = jnp.zeros((8, PW), F32)
        used[z] = 0
        return 0

    lax.fori_loop(0, zones, clear, 0)

    def patch(z, _):
        before = jnp.maximum(z - 1, 0)
        after = jnp.minimum(z + 1, zones - 1)
        value = table[z, 0:8, :]
        sides = []
        for row in (8, 9):
            low = jnp.broadcast_to(table[before, row : row + 1, :], (8, PW))
            high = jnp.broadcast_to(table[after, row : row + 1, :], (8, PW))
            sides.append(jnp.where(lane < EDGE, high, low))
        edges = jnp.where(sub < 4, sides[0], sides[1])
        at = jnp.clip(value.astype(jnp.int32) - int(MARK), 0, PW - 1)
        found = jnp.take_along_axis(edges, at, axis=1, mode="promise_in_bounds")
        full[z] = jnp.where(value >= MARK, found, value)
        return 0

    lax.fori_loop(0, zones, patch, 0, unroll=4)

    def pick(t, _):
        blob = blob_s[0, t]
        row = table[blob >> 6, 10:11, :]
        info[pl.ds(t, 1), :] = jnp.where((lane[0:1] & (BLOBS - 1)) == (blob & (BLOBS - 1)), row, 0.0)
        return 0

    lax.fori_loop(0, tiles, pick, 0, unroll=8)
    half = iota((PW, 2 * PW), 0) // BLOBS == iota((PW, 2 * PW), 1) // PW
    ranges[...] = exact_left(info[...], jnp.where(half, 1.0, 0.0).astype(BF16), NN)
    ones = jnp.ones((PW, PW), BF16)

    def positions(g):
        picked = [[], []]
        spans = ranges[pl.ds(pl.multiple_of(g * GROUP, GROUP), GROUP), :]
        for s in range(GROUP):
            t = g * GROUP + s
            zone = blob_s[0, t] >> 6
            start = jnp.broadcast_to(spans[s : s + 1, 0:PW], (SLOTS, PW))
            index = start + slot_f
            hits = [index == lane16 + float(PW * n) for n in range(4)]
            for p in range(2):
                value = jnp.zeros((SLOTS, PW), F32)
                for n in range(4):
                    row = full[zone, 4 * p + n : 4 * p + n + 1, :]
                    value = jnp.where(hits[n], jnp.broadcast_to(row, (SLOTS, PW)), value)
                picked[p].append(value)
        return exact_left(jnp.concatenate(picked[0] + picked[1], axis=0), ones, NN), spans

    def render(g, buf):
        base = g * (GROUP * PH)
        where, spans = positions(g)
        for i in range(PH):
            root = jnp.sqrt(weights[pl.ds(base + i, GROUP, stride=PH), :])
            roots[GROUP * i : GROUP * (i + 1), :] = root
            scaled = root * pixels[pl.ds(base + i, GROUP, stride=PH), :]
            high = scaled.astype(BF16).astype(F32)
            both = jnp.concatenate([high, scaled - high], axis=0)
            buf[256:272, PW * i : PW * (i + 1)] = both.astype(BF16)
        for s in range(GROUP):
            t = g * GROUP + s
            y = where[SLOTS * s : SLOTS * (s + 1)]
            x = where[128 + SLOTS * s : 128 + SLOTS * (s + 1)]
            count = jnp.broadcast_to(spans[s : s + 1, PW : 2 * PW], (SLOTS, PW))
            live = jnp.where(slot_f < count, 1.0, 0.0)
            dx = (lane16 - off_s[1, t]) - x
            dx = dx * dx
            scales = [inv_s[c, t] for c in range(3)]
            cols = [jnp.exp2(scales[c] * dx) * (live * amp_s[c, t]) for c in range(3)]
            for i in range(PH):
                dy = (float(i) - off_s[0, t]) - y
                dy = dy * dy
                total = None
                for c in range(3):
                    term = jnp.exp2(scales[c] * dy) * cols[c]
                    total = term if total is None else total + term
                row = GROUP * i + s
                total = total * jnp.broadcast_to(roots[row : row + 1, :], (SLOTS, PW))
                high = total.astype(BF16)
                low = (total - high.astype(F32)).astype(BF16)
                buf[SLOTS * s : SLOTS * (s + 1), PW * i : PW * (i + 1)] = low
                buf[128 + SLOTS * s : 128 + SLOTS * (s + 1), PW * i : PW * (i + 1)] = high

    def finish(g, buf):
        prod = dot(buf[128:272, :], buf[0:256, :], NT)
        cross = prod[0:128, 0:128]
        gram = prod[0:128, 128:256] + (cross + jnp.transpose(cross))
        rhs8 = prod[128:136, 128:256] + (prod[128:136, 0:128] + prod[136:144, 128:256])
        upper = jnp.zeros((8, PW), F32)
        lower = jnp.zeros((8, PW), F32)
        for s in range(GROUP):
            upper = jnp.where(spot == s, gram[SLOTS * s : SLOTS * s + 8], upper)
            lower = jnp.where(spot == s, gram[SLOTS * s + 8 : SLOTS * s + 16], lower)
        fold = jnp.where(entry < sub, pltpu.roll(lower, PW - 8, 1), upper)
        diag = jnp.sum(jnp.where(entry == sub + 8, lower, 0.0), axis=0, keepdims=True)
        rhs = jnp.sum(jnp.where(spot == sub, rhs8, 0.0), axis=0, keepdims=True)
        label = jnp.zeros((1, PW), F32)
        for s in range(GROUP):
            t = g * GROUP + s
            code = band_s[0, t] * BLOBS + (blob_s[0, t] & (BLOBS - 1)) + 1
            label = jnp.where(lane[0:1] == SLOTS * s, code.astype(F32), label)
        extra = jnp.where(sub == 0, rhs, jnp.where(sub == 1, diag + label, 0.0))
        for s in range(GROUP):
            t = g * GROUP + s
            zone = blob_s[0, t] >> 6
            place = used[zone]
            used[zone] = place + 1
            shift = SLOTS * (place - s)
            value = jnp.where(
                lane < 64,
                pltpu.roll(fold, (shift + 128) & 127, 1),
                pltpu.roll(extra, (shift + 192) & 127, 1),
            )
            mine = (spot & 3) == place
            out[zone] = jnp.where(mine, value, out[zone])

    groups = tiles // GROUP
    render(0, buf_a)

    def step(n, _):
        render(2 * n + 1, buf_b)
        finish(2 * n, buf_a)
        render(jnp.minimum(2 * n + 2, groups - 1), buf_a)
        finish(2 * n + 1, buf_b)
        return 0

    lax.fori_loop(0, groups // 2, step, 0)


def gather_kernel(got, out):
    zones = got.shape[0] // 8
    lane = iota((zones, PW), 1)
    spot = lane >> 4
    parts = [got[pl.ds(r, zones, stride=8), :] for r in range(8)]
    body = []
    for s in range(4):
        main = jnp.zeros((zones, PW), F32)
        for r in range(8):
            shift = (SLOTS * (r - s)) % PW
            moved = pltpu.roll(parts[r], shift, 1) if shift else parts[r]
            main = jnp.where(spot == r, moved, main)
        rhs = pltpu.roll(parts[0], (64 - SLOTS * s) % PW, 1)
        rest = pltpu.roll(parts[1], (64 + SLOTS - SLOTS * s) % PW, 1)
        extra = jnp.where(spot == 0, rhs, jnp.where(spot == 1, rest, 0.0))
        body.append(jnp.concatenate([main, extra], axis=1))
    values = jnp.concatenate(body, axis=0)
    label = values[:, PW + SLOTS : PW + SLOTS + 1]
    systems = out.shape[1]
    codes = iota((4 * zones, systems), 1).astype(F32) + 1.0
    onehot = jnp.where(label == codes, 1.0, 0.0).astype(BF16)
    total = exact_left(values, onehot, TN)
    out[...] = total[0 : out.shape[0]]


def solve_kernel(first, second, third, fourth, members, counts, own, before, after, left, right, xs):
    sums = (first[...] + second[...]) + (third[...] + fourth[...])
    width = sums.shape[1]
    left[...] = sums[:, 0:PW]
    right[...] = sums[:, PW:width]
    sub = iota((8, width), 0)

    def bcast(x, k):
        return jnp.broadcast_to(x[k : k + 1], (8, width))

    low_half = [None] * SLOTS
    high_half = [None] * SLOTS
    for k in range(8):
        low_half[k] = sums[SLOTS * k : SLOTS * k + 8, :] + jnp.where(sub == k, 1.0, 0.0)
        high_half[k] = sums[SLOTS * k + 8 : SLOTS * k + 16, :]
        corner = jnp.concatenate(
            [half[pl.ds(k, 8, stride=SLOTS), :] for half in (left, right)], axis=1
        )
        diag = bcast(sums[128 + SLOTS + 8 : 128 + SLOTS + 16, :], k) + 1.0
        high_half[8 + k] = jnp.where(sub == k, diag, corner)
    rhs = [sums[128:136, :], sums[136:144, :]]
    pivots = []
    values = []
    for k in range(SLOTS):
        halves = [low_half[k], high_half[k]] if k < 8 else [None, high_half[k]]
        inverse = 1.0 / bcast(halves[k // 8], k % 8)
        scaled = [None if h is None else h * inverse for h in halves]
        value = bcast(rhs[k // 8], k % 8)
        pivots.append(inverse)
        values.append(value)
        for h in range(2):
            if scaled[h] is not None:
                rhs[h] = rhs[h] - scaled[h] * value
        for j in range(k + 1, SLOTS):
            factor = bcast(scaled[j // 8], j % 8)
            if j < 8:
                low_half[j] = low_half[j] - factor * halves[0]
            high_half[j] = high_half[j] - factor * halves[1]
    x = [jnp.zeros((8, width), F32), jnp.zeros((8, width), F32)]
    for k in reversed(range(SLOTS)):
        acc = jnp.where(sub > k - 8, high_half[k] * x[1], 0.0)
        if k < 8:
            acc = acc + jnp.where(sub > k, low_half[k] * x[0], 0.0)
        solved = (values[k] - jnp.sum(acc, axis=0, keepdims=True)) * pivots[k]
        x[k // 8] = jnp.where(sub == k % 8, solved, x[k // 8])
    xs[0:8, :] = x[0]
    xs[8:16, :] = x[1]

    lane = iota((8, PW), 1)
    sub8 = iota((8, PW), 0)
    doubled = []
    for k in range(BANDS):
        tile = xs[:, PW * (k // 2) : PW * (k // 2 + 1)]
        turned = pltpu.roll(tile, 64, 1)
        wide = iota((SLOTS, PW), 1)
        doubled.append(
            jnp.where(wide < 64, tile, turned) if k % 2 == 0 else jnp.where(wide < 64, turned, tile)
        )
    pieces = []
    for n in range(8):
        piece = jnp.zeros((8, PW), F32)
        for k in range(BANDS):
            row = jnp.where(
                lane < 64,
                jnp.broadcast_to(doubled[k][2 * n : 2 * n + 1], (8, PW)),
                jnp.broadcast_to(doubled[k][2 * n + 1 : 2 * n + 2], (8, PW)),
            )
            piece = jnp.where(sub8 == k, row, piece)
        pieces.append(piece)
    flat = jnp.concatenate(pieces, axis=1)
    extent = SRC + 2 * EDGE
    columns = members[...].astype(F32)
    slots = iota((BLOBS, SLOTS), 1).astype(F32)
    columns = jnp.where(slots < counts[...], columns, -1.0)
    targets = iota((BLOBS, extent), 1)
    targets = jnp.where(targets < SRC, targets + EDGE, jnp.where(targets < SRC + EDGE, targets - SRC, targets))
    targets = targets.astype(F32)
    onehot = jnp.concatenate(
        [jnp.where(columns[:, j : j + 1] == targets, 1.0, 0.0).astype(BF16) for j in range(SLOTS)],
        axis=0,
    )
    fluxes = exact_left(flat, onehot, NN)
    own[...] = fluxes[:, 0:SRC]
    rim = fluxes[:, SRC:extent]
    before[...] = jnp.where(lane < EDGE, rim, 0.0)
    after[...] = jnp.where(lane < EDGE, 0.0, rim)


def edge_kernel(own, from_before, from_after, edge_rows, out):
    rim = pltpu.roll(from_before[...] + from_after[...], EDGE, 1)
    rows = edge_rows[...]
    targets = iota((2 * EDGE, SRC), 1)
    onehot = jnp.where(rows == targets, 1.0, 0.0).astype(BF16)
    out[...] = (own[...] + exact_left(rim, onehot, NN))[0:BANDS]


def call(kernel, out_shape, in_specs, scratch=(), out_specs=None):
    return pl.pallas_call(
        kernel,
        out_shape=out_shape,
        in_specs=in_specs,
        out_specs=VMEM if out_specs is None else out_specs,
        scratch_shapes=list(scratch),
        compiler_params=pltpu.CompilerParams(vmem_limit_bytes=48 * 1024 * 1024),
    )


def on_device(
    pixels,
    inv_var,
    tile_offset,
    psf_amp,
    psf_sigma,
    tile_blob,
    tile_band,
    source_pos,
    edge_rows,
    blob_members,
    sources_per_blob,
):
    zones = lax.axis_size("zone")
    bands = lax.axis_size("band")
    shape = jax.ShapeDtypeStruct
    counts = sources_per_blob.astype(F32)
    spread = call(table_kernel, shape((zones, TABLE_ROWS, PW), F32), [VMEM] * 4)(
        blob_members, counts.reshape(1, -1), source_pos, edge_rows.reshape(1, -1)
    )
    table = lax.all_to_all(spread, "zone", split_axis=0, concat_axis=0, tiled=True)
    inverse = -LOG2E * (0.5 / (psf_sigma * psf_sigma))
    tiles = pixels.shape[0]
    terms = call(
        tile_kernel,
        shape((zones, 8, PW), F32),
        [SMEM] * 5 + [VMEM] * 3,
        [
            pltpu.VMEM((272, PH * PW), BF16),
            pltpu.VMEM((272, PH * PW), BF16),
            pltpu.VMEM((GROUP * PH, PW), F32),
            pltpu.VMEM((zones, 8, PW), F32),
            pltpu.VMEM((tiles, PW), F32),
            pltpu.VMEM((tiles, 2 * PW), F32),
            pltpu.SMEM((zones,), jnp.int32),
        ],
    )(
        tile_blob.reshape(1, -1),
        tile_band.reshape(1, -1),
        tile_offset,
        psf_amp,
        inverse,
        table,
        pixels.reshape(tiles * PH, PW),
        inv_var.reshape(tiles * PH, PW),
    )
    got = lax.all_to_all(terms, "zone", split_axis=0, concat_axis=0, tiled=True)
    systems = call(gather_kernel, shape((160, 2 * PW), F32), [VMEM])(got.reshape(zones * 8, PW))
    others = [
        lax.ppermute(systems, "band", [(i, (i + k) % bands) for i in range(bands)])
        for k in range(1, bands)
    ]
    own, before, after = call(
        solve_kernel,
        (shape((8, SRC), F32), shape((8, PW), F32), shape((8, PW), F32)),
        [VMEM] * 6,
        [pltpu.VMEM((160, PW), F32), pltpu.VMEM((160, PW), F32), pltpu.VMEM((SLOTS, 2 * PW), F32)],
        (VMEM, VMEM, VMEM),
    )(systems, *others, blob_members, counts.reshape(-1, 1))
    up = [(i, i + 1) for i in range(zones - 1)]
    down = [(b, a) for a, b in up]
    from_before = lax.ppermute(after, "zone", up)
    from_after = lax.ppermute(before, "zone", down)
    return call(edge_kernel, shape((BANDS, SRC), F32), [VMEM] * 4)(
        own, from_before, from_after, edge_rows.reshape(-1, 1)
    )


def solution(mesh):
    tile = P(("zone", "band"))
    return jax.shard_map(
        on_device,
        mesh=mesh,
        in_specs=(
            P(("zone", "band"), None, None),
            P(("zone", "band"), None, None),
            P(None, ("zone", "band")),
            P(None, ("zone", "band")),
            P(None, ("zone", "band")),
            tile,
            tile,
            P(None, "zone"),
            P("zone"),
            P("zone", None),
            P("zone"),
        ),
        out_specs=P(None, "zone"),
        check_vma=False,
    )
```

```python
import functools

import jax
import jax.numpy as jnp
from jax import lax
from jax.experimental import pallas as pl
from jax.experimental.pallas import tpu as pltpu
from jax.sharding import PartitionSpec as P

BANDS = 3
SLOTS = 16
PH = 32
PW = 128
SRC = 512
BLOBS = 64
EDGE = 64
GROUP = 8
TABLE_ROWS = 16
MARK = 1000.0
LOG2E = 1.4426950408889634
F32 = jnp.float32
BF16 = jnp.bfloat16
NT = (((1,), (1,)), ((), ()))
NN = (((1,), (0,)), ((), ()))
TN = (((0,), (0,)), ((), ()))
VMEM = pl.BlockSpec(memory_space=pltpu.VMEM)
SMEM = pl.BlockSpec(memory_space=pltpu.SMEM)


def iota(shape, axis):
    return lax.broadcasted_iota(jnp.int32, shape, axis)


def three_parts(x):
    high = x.astype(BF16)
    rest = x - high.astype(F32)
    mid = rest.astype(BF16)
    low = (rest - mid.astype(F32)).astype(BF16)
    return high, mid, low


def dot(a, b, dims):
    return lax.dot_general(a, b, dims, preferred_element_type=F32)


def exact_left(x, onehot, dims):
    high, mid, low = three_parts(x)
    return (dot(low, onehot, dims) + dot(mid, onehot, dims)) + dot(high, onehot, dims)


def table_kernel(members, counts, source_pos, edge_rows, out):
    cnt = counts[...].astype(F32)
    above = iota((BLOBS, BLOBS), 0)
    beside = iota((BLOBS, BLOBS), 1)
    spread = jnp.broadcast_to(cnt, (BLOBS, BLOBS))
    start = jnp.sum(jnp.where(beside < above, spread, 0.0), axis=1, keepdims=True)
    own = jnp.sum(jnp.where(beside == above, spread, 0.0), axis=1, keepdims=True)
    start_row = jnp.sum(jnp.where(above == beside, start, 0.0), axis=0, keepdims=True)
    entry = iota((BLOBS, SRC), 1).astype(F32)
    inside = jnp.logical_and(entry >= start, entry < start + own)
    slot = jnp.sum(jnp.where(inside, entry - start, 0.0), axis=0, keepdims=True)
    picked = exact_left(members[...].astype(F32), inside.astype(BF16), NN)
    slot_ids = iota((SLOTS, SRC), 0).astype(F32)
    source = jnp.sum(jnp.where(slot_ids == slot, picked, 0.0), axis=0, keepdims=True)
    wanted = jnp.concatenate([source, edge_rows[...].astype(F32) + float(EDGE)], axis=1)
    width = SRC + 2 * EDGE
    row_ids = iota((SRC, width), 0).astype(F32) + float(EDGE)
    onehot = jnp.where(row_ids == wanted, 1.0, 0.0).astype(BF16)
    pos = jnp.concatenate([source_pos[...], jnp.zeros((6, SRC), F32)], axis=0)
    got = exact_left(pos, onehot, NN)
    lanes = iota((1, width), 1)
    mark = jnp.where(wanted < float(EDGE), wanted + (MARK + EDGE), wanted + (MARK - EDGE - SRC))
    outside = jnp.logical_or(wanted < float(EDGE), wanted >= float(EDGE + SRC))
    marked = jnp.logical_and(lanes < SRC, outside)
    got = jnp.where(marked, mark, got)
    rows = [got[p : p + 1, PW * n : PW * (n + 1)] for p in range(2) for n in range(4)]
    rows += [got[p : p + 1, SRC : SRC + PW] for p in range(2)]
    rows.append(jnp.concatenate([start_row, cnt], axis=1))
    rows.append(jnp.zeros((TABLE_ROWS - 11, PW), F32))
    table = jnp.concatenate(rows, axis=0)

    def write(z, _):
        out[z] = table
        return 0

    lax.fori_loop(0, out.shape[0], write, 0, unroll=8)


def prepare_kernel(pixels, weights, roots, scaled):
    def group(g, _):
        base = pl.multiple_of(g * (GROUP * PH), GROUP * PH)
        for i in range(PH):
            root = jnp.sqrt(weights[pl.ds(base + i, GROUP, stride=PH), :])
            roots[pl.ds(base + GROUP * i, GROUP), :] = root
            product = root * pixels[pl.ds(base + i, GROUP, stride=PH), :]
            high = product.astype(BF16).astype(F32)
            both = jnp.concatenate([high, product - high], axis=0)
            scaled[g, i // 2, :, PW * (i % 2) : PW * (i % 2 + 1)] = both.astype(BF16)
        return 0

    lax.fori_loop(0, scaled.shape[0], group, 0)


def place_kernel(code_s, table, places, counts, full, info, ranges):
    zones = table.shape[0]
    tiles = info.shape[0]
    lane = iota((8, PW), 1)
    sub = iota((8, PW), 0)
    lane16 = iota((SLOTS, PW), 1).astype(F32)
    slot_f = iota((SLOTS, PW), 0).astype(F32)

    def patch(z, _):
        before = jnp.maximum(z - 1, 0)
        after = jnp.minimum(z + 1, zones - 1)
        value = table[z, 0:8, :]
        sides = []
        for row in (8, 9):
            low = jnp.broadcast_to(table[before, row : row + 1, :], (8, PW))
            high = jnp.broadcast_to(table[after, row : row + 1, :], (8, PW))
            sides.append(jnp.where(lane < EDGE, high, low))
        edges = jnp.where(sub < 4, sides[0], sides[1])
        at = jnp.clip(value.astype(jnp.int32) - int(MARK), 0, PW - 1)
        found = jnp.take_along_axis(edges, at, axis=1, mode="promise_in_bounds")
        full[z] = jnp.where(value >= MARK, found, value)
        return 0

    lax.fori_loop(0, zones, patch, 0, unroll=8)

    def pick(t, _):
        blob = code_s[0, t] >> 2
        row = table[blob >> 6, 10:11, :]
        info[pl.ds(t, 1), :] = jnp.where((lane[0:1] & (BLOBS - 1)) == (blob & (BLOBS - 1)), row, 0.0)
        return 0

    lax.fori_loop(0, tiles, pick, 0, unroll=16)
    half = iota((PW, 2 * PW), 0) // BLOBS == iota((PW, 2 * PW), 1) // PW
    ranges[...] = exact_left(info[...], jnp.where(half, 1.0, 0.0).astype(BF16), NN)
    counts[...] = ranges[:, PW : 2 * PW]
    ones = jnp.ones((PW, PW), BF16)

    def positions(g, _):
        picked = [[], []]
        spans = ranges[pl.ds(pl.multiple_of(g * GROUP, GROUP), GROUP), :]
        for s in range(GROUP):
            t = g * GROUP + s
            zone = code_s[0, t] >> 8
            start = jnp.broadcast_to(spans[s : s + 1, 0:PW], (SLOTS, PW))
            index = start + slot_f
            hits = [index == lane16 + float(PW * n) for n in range(4)]
            for p in range(2):
                value = jnp.zeros((SLOTS, PW), F32)
                for n in range(4):
                    row = full[zone, 4 * p + n : 4 * p + n + 1, :]
                    value = jnp.where(hits[n], jnp.broadcast_to(row, (SLOTS, PW)), value)
                picked[p].append(value)
        places[g] = exact_left(jnp.concatenate(picked[0] + picked[1], axis=0), ones, NN)
        return 0

    lax.fori_loop(0, tiles // GROUP, positions, 0, unroll=2)


def tile_kernel(
    code_s,
    par_s,
    places,
    counts,
    roots,
    scaled,
    out,
    buf_a,
    buf_b,
    used,
):
    zones = out.shape[0]
    tiles = counts.shape[0]
    lane = iota((8, PW), 1)
    sub = iota((8, PW), 0)
    lane16 = iota((SLOTS, PW), 1).astype(F32)
    slot_f = iota((SLOTS, PW), 0).astype(F32)
    spot = lane >> 4
    entry = lane & (SLOTS - 1)

    def clear(z, _):
        out[z] = jnp.zeros((8, PW), F32)
        used[z] = 0
        return 0

    lax.fori_loop(0, zones, clear, 0)

    def store(g, buf, s, i, total):
        root = roots[pl.ds(GROUP * (PH * g + i) + s, 1), :]
        total = total * jnp.broadcast_to(root, (SLOTS, PW))
        high = total.astype(BF16)
        low = (total - high.astype(F32)).astype(BF16)
        first = pl.multiple_of(SLOTS * s, SLOTS)
        side = slice(PW * (i % 2), PW * (i % 2 + 1))
        buf[i // 2, pl.ds(first, SLOTS), side] = low
        buf[i // 2, pl.ds(128 + first, SLOTS), side] = high

    def render(g, s, buf, meanwhile):
        t = g * GROUP + s
        first = pl.multiple_of(SLOTS * s, SLOTS)
        y = places[g, pl.ds(first, SLOTS), :]
        x = places[g, pl.ds(128 + first, SLOTS), :]
        count = jnp.broadcast_to(counts[pl.ds(t, 1), :], (SLOTS, PW))
        live = jnp.where(slot_f < count, 1.0, 0.0)
        dx = (lane16 - par_s[1, t]) - x
        dx = dx * dx
        dy = (float(PH // 2) - par_s[0, t]) - y
        flat = jnp.zeros((8, PW), F32)
        here, up, down, turn = [], [], [], []
        for c in range(3):
            scale = par_s[5 + c, t]
            col = jnp.exp2(scale * dx) * (live * par_s[2 + c, t])
            here.append(jnp.exp2(scale * (dy * dy)) * col)
            up.append(jnp.exp2(scale * (2.0 * dy + 1.0)))
            down.append(jnp.exp2(scale * (1.0 - 2.0 * dy)))
            step = jnp.exp2(flat + 2.0 * scale)
            turn.append(jnp.concatenate([step, step], axis=0))
        store(g, buf, s, PH // 2, (here[0] + here[1]) + here[2])
        above, below = list(here), list(here)
        for n in range(1, PH // 2 + 1):
            if n in meanwhile:
                meanwhile[n]()
            for c in range(3):
                below[c] = below[c] * down[c]
                down[c] = down[c] * turn[c]
            store(g, buf, s, PH // 2 - n, (below[0] + below[1]) + below[2])
            if n < PH // 2:
                for c in range(3):
                    above[c] = above[c] * up[c]
                    up[c] = up[c] * turn[c]
                store(g, buf, s, PH // 2 + n, (above[0] + above[1]) + above[2])

    def finish(g, prod, sides):
        cross = prod[0:128, 0:128]
        gram = prod[0:128, 128:256] + (cross + jnp.transpose(cross))
        rhs8 = sides[0:8, 128:256] + (sides[0:8, 0:128] + sides[8:16, 128:256])
        upper = jnp.zeros((8, PW), F32)
        lower = jnp.zeros((8, PW), F32)
        for s in range(GROUP):
            upper = jnp.where(spot == s, gram[SLOTS * s : SLOTS * s + 8], upper)
            lower = jnp.where(spot == s, gram[SLOTS * s + 8 : SLOTS * s + 16], lower)
        fold = jnp.where(entry < sub, pltpu.roll(lower, PW - 8, 1), upper)
        diag = jnp.sum(jnp.where(entry == sub + 8, lower, 0.0), axis=0, keepdims=True)
        rhs = jnp.sum(jnp.where(spot == sub, rhs8, 0.0), axis=0, keepdims=True)
        label = jnp.zeros((1, PW), F32)
        for s in range(GROUP):
            t = g * GROUP + s
            code = (code_s[0, t] & 3) * BLOBS + ((code_s[0, t] >> 2) & (BLOBS - 1)) + 1
            label = jnp.where(lane[0:1] == SLOTS * s, code.astype(F32), label)
        extra = jnp.where(sub == 0, rhs, jnp.where(sub == 1, diag + label, 0.0))
        for s in range(GROUP):
            t = g * GROUP + s
            zone = code_s[0, t] >> 8
            place = used[zone]
            used[zone] = place + 1
            shift = SLOTS * (place - s)
            value = jnp.where(
                lane < 64,
                pltpu.roll(fold, (shift + 128) & 127, 1),
                pltpu.roll(extra, (shift + 192) & 127, 1),
            )
            mine = (spot & 3) == place
            out[zone] = jnp.where(mine, value, out[zone])

    def run(sum_a, sum_b, rhs_a, rhs_b):
        def load(buf, k, unit, stage):
            pltpu.matmul_push_rhs(buf[k, 0:256, :], stage, unit, transpose=True)

        def multiply(g, buf, k, unit, stage):
            pltpu.matmul_acc_lhs((sum_a, sum_b)[unit], buf[k, 128:256, :], load_staged_rhs=stage)
            pltpu.matmul_acc_lhs((rhs_a, rhs_b)[unit], scaled[g, k])

        def total():
            gram = pltpu.matmul_pop(sum_a) + pltpu.matmul_pop(sum_b)
            return gram, pltpu.matmul_pop(rhs_a) + pltpu.matmul_pop(rhs_b)

        def both(g, buf, before):

            def pair(u, _):
                steps = [{}, {}]
                if before is not None:
                    for stage in range(2):
                        for unit in range(2):
                            work = (4 * u + 2 * stage + unit, unit, stage)
                            n = 2 * (2 * stage + unit) + 1
                            steps[0][n] = functools.partial(load, before[1], *work)
                            n = 8 * (1 - stage) + 2 * unit + 1
                            steps[stage][n] = functools.partial(multiply, *before, *work)
                for half in range(2):
                    render(g, 2 * u + half, buf, steps[half])
                return 0

            lax.fori_loop(0, GROUP // 2, pair, 0, unroll=2)
            if before is not None:
                finish(before[0], *total())

        def last(g, buf):
            for k in range(2 * GROUP):
                load(buf, k, k % 2, k // 2 % 2)
                multiply(g, buf, k, k % 2, k // 2 % 2)
            finish(g, *total())

        groups = tiles // GROUP
        both(0, buf_a, None)

        def step(n, _):
            both(2 * n + 1, buf_b, (2 * n, buf_a))
            both(2 * n + 2, buf_a, (2 * n + 1, buf_b))
            return 0

        lax.fori_loop(0, groups // 2 - 1, step, 0)
        both(groups - 1, buf_b, (groups - 2, buf_a))
        last(groups - 1, buf_b)

    shapes = [pltpu.ACC(unit)((rows, 256), F32) for rows in (128, 16) for unit in range(2)]
    pl.run_scoped(run, *shapes)


def gather_kernel(got, out):
    zones = got.shape[0] // 8
    lane = iota((zones, PW), 1)
    spot = lane >> 4
    parts = [got[pl.ds(r, zones, stride=8), :] for r in range(8)]
    body = []
    for s in range(4):
        main = jnp.zeros((zones, PW), F32)
        for r in range(8):
            shift = (SLOTS * (r - s)) % PW
            moved = pltpu.roll(parts[r], shift, 1) if shift else parts[r]
            main = jnp.where(spot == r, moved, main)
        rhs = pltpu.roll(parts[0], (64 - SLOTS * s) % PW, 1)
        rest = pltpu.roll(parts[1], (64 + SLOTS - SLOTS * s) % PW, 1)
        extra = jnp.where(spot == 0, rhs, jnp.where(spot == 1, rest, 0.0))
        body.append(jnp.concatenate([main, extra], axis=1))
    values = jnp.concatenate(body, axis=0)
    label = values[:, PW + SLOTS : PW + SLOTS + 1]
    systems = 2 * PW
    codes = iota((4 * zones, systems), 1).astype(F32) + 1.0
    onehot = jnp.where(label == codes, 1.0, 0.0).astype(BF16)
    total = exact_left(values, onehot, TN)
    out[0:160] = total[0:160, 0:PW]
    turned = pltpu.roll(total[80:160, PW:systems], EDGE, 1)
    out[160:240] = jnp.where(iota((80, PW), 1) < EDGE, total[0:80, PW:systems], turned)


def solve_kernel(first, second, third, fourth, members, counts, own, before, after, left, right, xs):
    both = (first[...] + second[...]) + (third[...] + fourth[...])
    width = 2 * PW
    left[...] = both[0:160]
    right[0:80] = both[160:240]
    right[80:160] = pltpu.roll(both[160:240], EDGE, 1)
    sums = jnp.concatenate([left[...], right[...]], axis=1)
    sub = iota((8, width), 0)

    def bcast(x, k):
        return jnp.broadcast_to(x[k : k + 1], (8, width))

    low_half = [None] * SLOTS
    high_half = [None] * SLOTS
    for k in range(8):
        low_half[k] = sums[SLOTS * k : SLOTS * k + 8, :] + jnp.where(sub == k, 1.0, 0.0)
        high_half[k] = sums[SLOTS * k + 8 : SLOTS * k + 16, :]
        corner = jnp.concatenate(
            [half[pl.ds(k, 8, stride=SLOTS), :] for half in (left, right)], axis=1
        )
        diag = bcast(sums[128 + SLOTS + 8 : 128 + SLOTS + 16, :], k) + 1.0
        high_half[8 + k] = jnp.where(sub == k, diag, corner)
    rhs = [sums[128:136, :], sums[136:144, :]]
    pivots = []
    values = []
    for k in range(SLOTS):
        halves = [low_half[k], high_half[k]] if k < 8 else [None, high_half[k]]
        inverse = 1.0 / bcast(halves[k // 8], k % 8)
        scaled = [None if h is None else h * inverse for h in halves]
        value = bcast(rhs[k // 8], k % 8)
        pivots.append(inverse)
        values.append(value)
        for h in range(2):
            if scaled[h] is not None:
                rhs[h] = rhs[h] - scaled[h] * value
        for j in range(k + 1, SLOTS):
            factor = bcast(scaled[j // 8], j % 8)
            if j < 8:
                low_half[j] = low_half[j] - factor * halves[0]
            high_half[j] = high_half[j] - factor * halves[1]
    x = [jnp.zeros((8, width), F32), jnp.zeros((8, width), F32)]
    for k in reversed(range(SLOTS)):
        acc = jnp.where(sub > k - 8, high_half[k] * x[1], 0.0)
        if k < 8:
            acc = acc + jnp.where(sub > k, low_half[k] * x[0], 0.0)
        solved = (values[k] - jnp.sum(acc, axis=0, keepdims=True)) * pivots[k]
        x[k // 8] = jnp.where(sub == k % 8, solved, x[k // 8])
    xs[0:8, :] = x[0]
    xs[8:16, :] = x[1]

    lane = iota((8, PW), 1)
    sub8 = iota((8, PW), 0)
    doubled = []
    for k in range(BANDS):
        tile = xs[:, PW * (k // 2) : PW * (k // 2 + 1)]
        turned = pltpu.roll(tile, 64, 1)
        wide = iota((SLOTS, PW), 1)
        doubled.append(
            jnp.where(wide < 64, tile, turned) if k % 2 == 0 else jnp.where(wide < 64, turned, tile)
        )
    pieces = []
    for n in range(8):
        piece = jnp.zeros((8, PW), F32)
        for k in range(BANDS):
            row = jnp.where(
                lane < 64,
                jnp.broadcast_to(doubled[k][2 * n : 2 * n + 1], (8, PW)),
                jnp.broadcast_to(doubled[k][2 * n + 1 : 2 * n + 2], (8, PW)),
            )
            piece = jnp.where(sub8 == k, row, piece)
        pieces.append(piece)
    flat = jnp.concatenate(pieces, axis=1)
    extent = SRC + 2 * EDGE
    slots = iota((SLOTS, BLOBS), 0)
    columns = jnp.transpose(jnp.where(slots < counts[...], members[...], -1).astype(F32))
    targets = iota((BLOBS, extent), 1)
    targets = jnp.where(targets < SRC, targets + EDGE, jnp.where(targets < SRC + EDGE, targets - SRC, targets))
    targets = targets.astype(F32)
    onehot = jnp.concatenate(
        [jnp.where(columns[:, j : j + 1] == targets, 1.0, 0.0).astype(BF16) for j in range(SLOTS)],
        axis=0,
    )
    fluxes = exact_left(flat, onehot, NN)
    own[...] = fluxes[:, 0:SRC]
    rim = fluxes[:, SRC:extent]
    before[...] = jnp.where(lane < EDGE, rim, 0.0)
    after[...] = jnp.where(lane < EDGE, 0.0, rim)


def edge_kernel(own, from_before, from_after, edge_rows, out):
    rim = pltpu.roll(from_before[...] + from_after[...], EDGE, 1)
    rows = edge_rows[...]
    targets = iota((2 * EDGE, SRC), 1)
    onehot = jnp.where(rows == targets, 1.0, 0.0).astype(BF16)
    out[...] = (own[...] + exact_left(rim, onehot, NN))[0:BANDS]


def call(kernel, out_shape, in_specs, scratch=(), out_specs=None):
    return pl.pallas_call(
        kernel,
        out_shape=out_shape,
        in_specs=in_specs,
        out_specs=VMEM if out_specs is None else out_specs,
        scratch_shapes=list(scratch),
        compiler_params=pltpu.CompilerParams(vmem_limit_bytes=48 * 1024 * 1024),
    )


def on_device(
    pixels,
    inv_var,
    tile_offset,
    psf_amp,
    psf_sigma,
    tile_blob,
    tile_band,
    source_pos,
    edge_rows,
    blob_members,
    sources_per_blob,
):
    zones = lax.axis_size("zone")
    bands = lax.axis_size("band")
    shape = jax.ShapeDtypeStruct
    counts = sources_per_blob.reshape(1, -1)
    members = jnp.transpose(blob_members)
    spread = call(table_kernel, shape((zones, TABLE_ROWS, PW), F32), [VMEM] * 4)(
        members, counts, source_pos, edge_rows.reshape(1, -1)
    )
    table = lax.all_to_all(spread, "zone", split_axis=0, concat_axis=0, tiled=True)
    tiles = pixels.shape[0]
    groups = tiles // GROUP
    steps = 4
    rows = pl.BlockSpec((tiles * PH // steps, PW), lambda n: (n, 0))
    roots, scaled = pl.pallas_call(
        prepare_kernel,
        grid=(steps,),
        out_shape=(
            shape((tiles * PH, PW), F32),
            shape((groups, PH // 2, 2 * GROUP, 2 * PW), BF16),
        ),
        in_specs=[rows, rows],
        out_specs=(
            rows,
            pl.BlockSpec((groups // steps, PH // 2, 2 * GROUP, 2 * PW), lambda n: (n, 0, 0, 0)),
        ),
        compiler_params=pltpu.CompilerParams(vmem_limit_bytes=48 * 1024 * 1024),
    )(pixels.reshape(tiles * PH, PW), inv_var.reshape(tiles * PH, PW))
    inverse = -LOG2E * (0.5 / (psf_sigma * psf_sigma))
    numbers = jnp.concatenate([tile_offset, psf_amp, inverse], axis=0)
    codes = (tile_blob * 4 + tile_band).reshape(1, -1)
    places, live_counts = call(
        place_kernel,
        (shape((groups, 2 * PW, PW), F32), shape((tiles, PW), F32)),
        [SMEM, VMEM],
        [
            pltpu.VMEM((zones, 8, PW), F32),
            pltpu.VMEM((tiles, PW), F32),
            pltpu.VMEM((tiles, 2 * PW), F32),
        ],
        (VMEM, VMEM),
    )(codes, table)
    terms = call(
        tile_kernel,
        shape((zones, 8, PW), F32),
        [SMEM] * 2 + [VMEM] * 4,
        [
            pltpu.VMEM((PH // 2, 2 * PW, 2 * PW), BF16),
            pltpu.VMEM((PH // 2, 2 * PW, 2 * PW), BF16),
            pltpu.SMEM((zones,), jnp.int32),
        ],
    )(codes, numbers, places, live_counts, roots, scaled)
    got = lax.all_to_all(terms, "zone", split_axis=0, concat_axis=0, tiled=True)
    systems = call(gather_kernel, shape((240, PW), F32), [VMEM])(got.reshape(zones * 8, PW))
    others = [
        lax.ppermute(systems, "band", [(i, (i + k) % bands) for i in range(bands)])
        for k in range(1, bands)
    ]
    own, before, after = call(
        solve_kernel,
        (shape((8, SRC), F32), shape((8, PW), F32), shape((8, PW), F32)),
        [VMEM] * 6,
        [pltpu.VMEM((160, PW), F32), pltpu.VMEM((160, PW), F32), pltpu.VMEM((SLOTS, 2 * PW), F32)],
        (VMEM, VMEM, VMEM),
    )(systems, *others, members, counts)
    up = [(i, i + 1) for i in range(zones - 1)]
    down = [(b, a) for a, b in up]
    from_before = lax.ppermute(after, "zone", up)
    from_after = lax.ppermute(before, "zone", down)
    return call(edge_kernel, shape((BANDS, SRC), F32), [VMEM] * 4)(
        own, from_before, from_after, edge_rows.reshape(-1, 1)
    )


def solution(mesh):
    tile = P(("zone", "band"))
    return jax.shard_map(
        on_device,
        mesh=mesh,
        in_specs=(
            P(("zone", "band"), None, None),
            P(("zone", "band"), None, None),
            P(None, ("zone", "band")),
            P(None, ("zone", "band")),
            P(None, ("zone", "band")),
            tile,
            tile,
            P(None, "zone"),
            P("zone"),
            P("zone", None),
            P("zone"),
        ),
        out_specs=P(None, "zone"),
        check_vma=False,
    )
```

```python
import functools

import jax
import jax.numpy as jnp
from jax import lax
from jax.experimental import pallas as pl
from jax.experimental.pallas import tpu as pltpu
from jax.sharding import PartitionSpec as P

BANDS = 3
SLOTS = 16
PH = 32
PW = 128
SRC = 512
BLOBS = 64
EDGE = 64
GROUP = 8
TABLE_ROWS = 16
MARK = 1000.0
LOG2E = 1.4426950408889634
F32 = jnp.float32
BF16 = jnp.bfloat16
NT = (((1,), (1,)), ((), ()))
NN = (((1,), (0,)), ((), ()))
TN = (((0,), (0,)), ((), ()))
VMEM = pl.BlockSpec(memory_space=pltpu.VMEM)
SMEM = pl.BlockSpec(memory_space=pltpu.SMEM)


def iota(shape, axis):
    return lax.broadcasted_iota(jnp.int32, shape, axis)


def three_parts(x):
    high = x.astype(BF16)
    rest = x - high.astype(F32)
    mid = rest.astype(BF16)
    low = (rest - mid.astype(F32)).astype(BF16)
    return high, mid, low


def dot(a, b, dims):
    return lax.dot_general(a, b, dims, preferred_element_type=F32)


def exact_left(x, onehot, dims):
    high, mid, low = three_parts(x)
    return (dot(low, onehot, dims) + dot(mid, onehot, dims)) + dot(high, onehot, dims)


def table_kernel(members, counts, source_pos, edge_rows, out):
    cnt = counts[...].astype(F32)
    above = iota((BLOBS, BLOBS), 0)
    beside = iota((BLOBS, BLOBS), 1)
    spread = jnp.broadcast_to(cnt, (BLOBS, BLOBS))
    start = jnp.sum(jnp.where(beside < above, spread, 0.0), axis=1, keepdims=True)
    own = jnp.sum(jnp.where(beside == above, spread, 0.0), axis=1, keepdims=True)
    start_row = jnp.sum(jnp.where(above == beside, start, 0.0), axis=0, keepdims=True)
    entry = iota((BLOBS, SRC), 1).astype(F32)
    inside = jnp.logical_and(entry >= start, entry < start + own)
    slot = jnp.sum(jnp.where(inside, entry - start, 0.0), axis=0, keepdims=True)
    picked = exact_left(members[...].astype(F32), inside.astype(BF16), NN)
    slot_ids = iota((SLOTS, SRC), 0).astype(F32)
    source = jnp.sum(jnp.where(slot_ids == slot, picked, 0.0), axis=0, keepdims=True)
    wanted = jnp.concatenate([source, edge_rows[...].astype(F32) + float(EDGE)], axis=1)
    width = SRC + 2 * EDGE
    row_ids = iota((SRC, width), 0).astype(F32) + float(EDGE)
    onehot = jnp.where(row_ids == wanted, 1.0, 0.0).astype(BF16)
    pos = jnp.concatenate([source_pos[...], jnp.zeros((6, SRC), F32)], axis=0)
    got = exact_left(pos, onehot, NN)
    lanes = iota((1, width), 1)
    mark = jnp.where(wanted < float(EDGE), wanted + (MARK + EDGE), wanted + (MARK - EDGE - SRC))
    outside = jnp.logical_or(wanted < float(EDGE), wanted >= float(EDGE + SRC))
    marked = jnp.logical_and(lanes < SRC, outside)
    got = jnp.where(marked, mark, got)
    rows = [got[p : p + 1, PW * n : PW * (n + 1)] for p in range(2) for n in range(4)]
    rows += [got[p : p + 1, SRC : SRC + PW] for p in range(2)]
    rows.append(jnp.concatenate([start_row, cnt], axis=1))
    rows.append(jnp.zeros((TABLE_ROWS - 11, PW), F32))
    table = jnp.concatenate(rows, axis=0)

    def write(z, _):
        out[z] = table
        return 0

    lax.fori_loop(0, out.shape[0], write, 0, unroll=8)


def prepare_kernel(pixels, weights, roots, scaled):
    def group(g, _):
        base = pl.multiple_of(g * (GROUP * PH), GROUP * PH)
        for i in range(PH):
            root = jnp.sqrt(weights[pl.ds(base + i, GROUP, stride=PH), :])
            roots[pl.ds(base + GROUP * i, GROUP), :] = root
            product = root * pixels[pl.ds(base + i, GROUP, stride=PH), :]
            high = product.astype(BF16).astype(F32)
            both = jnp.concatenate([high, product - high], axis=0)
            scaled[g, i // 2, :, PW * (i % 2) : PW * (i % 2 + 1)] = both.astype(BF16)
        return 0

    lax.fori_loop(0, scaled.shape[0], group, 0)


def place_kernel(code_s, table, places, counts, full, info, ranges):
    zones = table.shape[0]
    tiles = info.shape[0]
    lane = iota((8, PW), 1)
    sub = iota((8, PW), 0)
    lane16 = iota((SLOTS, PW), 1).astype(F32)
    slot_f = iota((SLOTS, PW), 0).astype(F32)

    def patch(z, _):
        before = jnp.maximum(z - 1, 0)
        after = jnp.minimum(z + 1, zones - 1)
        value = table[z, 0:8, :]
        sides = []
        for row in (8, 9):
            low = jnp.broadcast_to(table[before, row : row + 1, :], (8, PW))
            high = jnp.broadcast_to(table[after, row : row + 1, :], (8, PW))
            sides.append(jnp.where(lane < EDGE, high, low))
        edges = jnp.where(sub < 4, sides[0], sides[1])
        at = jnp.clip(value.astype(jnp.int32) - int(MARK), 0, PW - 1)
        found = jnp.take_along_axis(edges, at, axis=1, mode="promise_in_bounds")
        full[z] = jnp.where(value >= MARK, found, value)
        return 0

    lax.fori_loop(0, zones, patch, 0, unroll=8)

    def pick(t, _):
        blob = code_s[0, t] >> 2
        row = table[blob >> 6, 10:11, :]
        info[pl.ds(t, 1), :] = jnp.where((lane[0:1] & (BLOBS - 1)) == (blob & (BLOBS - 1)), row, 0.0)
        return 0

    lax.fori_loop(0, tiles, pick, 0, unroll=16)
    half = iota((PW, 2 * PW), 0) // BLOBS == iota((PW, 2 * PW), 1) // PW
    ranges[...] = exact_left(info[...], jnp.where(half, 1.0, 0.0).astype(BF16), NN)
    counts[...] = ranges[:, PW : 2 * PW]
    ones = jnp.ones((PW, PW), BF16)

    def positions(g, _):
        picked = [[], []]
        spans = ranges[pl.ds(pl.multiple_of(g * GROUP, GROUP), GROUP), :]
        for s in range(GROUP):
            t = g * GROUP + s
            zone = code_s[0, t] >> 8
            start = jnp.broadcast_to(spans[s : s + 1, 0:PW], (SLOTS, PW))
            index = start + slot_f
            hits = [index == lane16 + float(PW * n) for n in range(4)]
            for p in range(2):
                value = jnp.zeros((SLOTS, PW), F32)
                for n in range(4):
                    row = full[zone, 4 * p + n : 4 * p + n + 1, :]
                    value = jnp.where(hits[n], jnp.broadcast_to(row, (SLOTS, PW)), value)
                picked[p].append(value)
        places[g] = exact_left(jnp.concatenate(picked[0] + picked[1], axis=0), ones, NN)
        return 0

    lax.fori_loop(0, tiles // GROUP, positions, 0, unroll=2)


def tile_kernel(
    code_s,
    par_s,
    places,
    counts,
    roots,
    scaled,
    out,
    buf_a,
    buf_b,
    used,
):
    zones = out.shape[0]
    tiles = counts.shape[0]
    lane = iota((8, PW), 1)
    sub = iota((8, PW), 0)
    lane16 = iota((SLOTS, PW), 1).astype(F32)
    slot_f = iota((SLOTS, PW), 0).astype(F32)
    spot = lane >> 4
    entry = lane & (SLOTS - 1)

    def clear(z, _):
        out[z] = jnp.zeros((8, PW), F32)
        used[z] = 0
        return 0

    lax.fori_loop(0, zones, clear, 0)

    def store(g, buf, s, i, total):
        root = roots[pl.ds(GROUP * (PH * g + i) + s, 1), :]
        total = total * jnp.broadcast_to(root, (SLOTS, PW))
        high = total.astype(BF16)
        low = (total - high.astype(F32)).astype(BF16)
        first = pl.multiple_of(SLOTS * s, SLOTS)
        side = slice(PW * (i % 2), PW * (i % 2 + 1))
        buf[i // 2, pl.ds(first, SLOTS), side] = low
        buf[i // 2, pl.ds(128 + first, SLOTS), side] = high

    def render(g, s, buf, meanwhile):
        t = g * GROUP + s
        first = pl.multiple_of(SLOTS * s, SLOTS)
        y = places[g, pl.ds(first, SLOTS), :]
        x = places[g, pl.ds(128 + first, SLOTS), :]
        count = jnp.broadcast_to(counts[pl.ds(t, 1), :], (SLOTS, PW))
        live = jnp.where(slot_f < count, 1.0, 0.0)
        dx = (lane16 - par_s[1, t]) - x
        dx = dx * dx
        dy = (float(PH // 2) - par_s[0, t]) - y
        flat = jnp.zeros((8, PW), F32)
        here, up, down, turn = [], [], [], []
        for c in range(3):
            scale = par_s[5 + c, t]
            col = jnp.exp2(scale * dx) * (live * par_s[2 + c, t])
            here.append(jnp.exp2(scale * (dy * dy)) * col)
            up.append(jnp.exp2(scale * (2.0 * dy + 1.0)))
            down.append(jnp.exp2(scale * (1.0 - 2.0 * dy)))
            step = jnp.exp2(flat + 2.0 * scale)
            turn.append(jnp.concatenate([step, step], axis=0))
        store(g, buf, s, PH // 2, (here[0] + here[1]) + here[2])
        above, below = list(here), list(here)
        for n in range(1, PH // 2 + 1):
            if n in meanwhile:
                meanwhile[n]()
            for c in range(3):
                below[c] = below[c] * down[c]
                down[c] = down[c] * turn[c]
            store(g, buf, s, PH // 2 - n, (below[0] + below[1]) + below[2])
            if n < PH // 2:
                for c in range(3):
                    above[c] = above[c] * up[c]
                    up[c] = up[c] * turn[c]
                store(g, buf, s, PH // 2 + n, (above[0] + above[1]) + above[2])

    def finish(g, prod, sides):
        cross = prod[0:128, 0:128]
        gram = prod[0:128, 128:256] + (cross + jnp.transpose(cross))
        rhs8 = sides[0:8, 128:256] + (sides[0:8, 0:128] + sides[8:16, 128:256])
        upper = jnp.zeros((8, PW), F32)
        lower = jnp.zeros((8, PW), F32)
        for s in range(GROUP):
            upper = jnp.where(spot == s, gram[SLOTS * s : SLOTS * s + 8], upper)
            lower = jnp.where(spot == s, gram[SLOTS * s + 8 : SLOTS * s + 16], lower)
        fold = jnp.where(entry < sub, pltpu.roll(lower, PW - 8, 1), upper)
        diag = jnp.sum(jnp.where(entry == sub + 8, lower, 0.0), axis=0, keepdims=True)
        rhs = jnp.sum(jnp.where(spot == sub, rhs8, 0.0), axis=0, keepdims=True)
        label = jnp.zeros((1, PW), F32)
        for s in range(GROUP):
            t = g * GROUP + s
            code = (code_s[0, t] & 3) * BLOBS + ((code_s[0, t] >> 2) & (BLOBS - 1)) + 1
            label = jnp.where(lane[0:1] == SLOTS * s, code.astype(F32), label)
        extra = jnp.where(sub == 0, rhs, jnp.where(sub == 1, diag + label, 0.0))
        for s in range(GROUP):
            t = g * GROUP + s
            zone = code_s[0, t] >> 8
            place = used[zone]
            used[zone] = place + 1
            shift = SLOTS * (place - s)
            value = jnp.where(
                lane < 64,
                pltpu.roll(fold, (shift + 128) & 127, 1),
                pltpu.roll(extra, (shift + 192) & 127, 1),
            )
            mine = (spot & 3) == place
            out[zone] = jnp.where(mine, value, out[zone])

    def run(sum_a, sum_b, rhs_a, rhs_b):
        def load(buf, k, unit, stage):
            pltpu.matmul_push_rhs(buf[k, 0:256, :], stage, unit, transpose=True)

        def multiply(g, buf, k, unit, stage):
            pltpu.matmul_acc_lhs((sum_a, sum_b)[unit], buf[k, 128:256, :], load_staged_rhs=stage)
            pltpu.matmul_acc_lhs((rhs_a, rhs_b)[unit], scaled[g, k])

        def total():
            gram = pltpu.matmul_pop(sum_a) + pltpu.matmul_pop(sum_b)
            return gram, pltpu.matmul_pop(rhs_a) + pltpu.matmul_pop(rhs_b)

        def both(g, buf, before, done):

            def pair(u, _):
                steps = [{}, {}]
                if before is not None:
                    for stage in range(2):
                        for unit in range(2):
                            work = (4 * u + 2 * stage + unit, unit, stage)
                            n = 2 * (2 * stage + unit) + 1
                            steps[0][n] = functools.partial(load, before[1], *work)
                            n = 8 * (1 - stage) + 2 * unit + 1
                            steps[stage][n] = functools.partial(multiply, *before, *work)
                for half in range(2):
                    render(g, 2 * u + half, buf, steps[half])
                return 0

            if done is not None:
                finish(done, *total())
            pair(jnp.int32(0), 0)
            lax.fori_loop(1, GROUP // 2, pair, 0)

        def last(g, buf):
            for k in range(2 * GROUP):
                load(buf, k, k % 2, k // 2 % 2)
                multiply(g, buf, k, k % 2, k // 2 % 2)
            finish(g, *total())

        groups = tiles // GROUP
        both(0, buf_a, None, None)
        both(1, buf_b, (0, buf_a), None)

        def step(n, _):
            both(2 * n, buf_a, (2 * n - 1, buf_b), 2 * n - 2)
            both(2 * n + 1, buf_b, (2 * n, buf_a), 2 * n - 1)
            return 0

        lax.fori_loop(1, groups // 2, step, 0)
        finish(groups - 2, *total())
        last(groups - 1, buf_b)

    shapes = [pltpu.ACC(unit)((rows, 256), F32) for rows in (128, 16) for unit in range(2)]
    pl.run_scoped(run, *shapes)


def gather_kernel(got, out):
    zones = got.shape[0] // 8
    lane = iota((zones, PW), 1)
    spot = lane >> 4
    parts = [got[pl.ds(r, zones, stride=8), :] for r in range(8)]
    body = []
    for s in range(4):
        main = jnp.zeros((zones, PW), F32)
        for r in range(8):
            shift = (SLOTS * (r - s)) % PW
            moved = pltpu.roll(parts[r], shift, 1) if shift else parts[r]
            main = jnp.where(spot == r, moved, main)
        rhs = pltpu.roll(parts[0], (64 - SLOTS * s) % PW, 1)
        rest = pltpu.roll(parts[1], (64 + SLOTS - SLOTS * s) % PW, 1)
        extra = jnp.where(spot == 0, rhs, jnp.where(spot == 1, rest, 0.0))
        body.append(jnp.concatenate([main, extra], axis=1))
    values = jnp.concatenate(body, axis=0)
    label = values[:, PW + SLOTS : PW + SLOTS + 1]
    systems = 2 * PW
    codes = iota((4 * zones, systems), 1).astype(F32) + 1.0
    onehot = jnp.where(label == codes, 1.0, 0.0).astype(BF16)
    total = exact_left(values, onehot, TN)
    out[0:160] = total[0:160, 0:PW]
    turned = pltpu.roll(total[80:160, PW:systems], EDGE, 1)
    out[160:240] = jnp.where(iota((80, PW), 1) < EDGE, total[0:80, PW:systems], turned)


def solve_kernel(first, second, third, fourth, members, counts, own, before, after, left, right, xs):
    both = (first[...] + second[...]) + (third[...] + fourth[...])
    width = 2 * PW
    left[...] = both[0:160]
    right[0:80] = both[160:240]
    right[80:160] = pltpu.roll(both[160:240], EDGE, 1)
    sums = jnp.concatenate([left[...], right[...]], axis=1)
    sub = iota((8, width), 0)

    def bcast(x, k):
        return jnp.broadcast_to(x[k : k + 1], (8, width))

    low_half = [None] * SLOTS
    high_half = [None] * SLOTS
    for k in range(8):
        low_half[k] = sums[SLOTS * k : SLOTS * k + 8, :] + jnp.where(sub == k, 1.0, 0.0)
        high_half[k] = sums[SLOTS * k + 8 : SLOTS * k + 16, :]
        corner = jnp.concatenate(
            [half[pl.ds(k, 8, stride=SLOTS), :] for half in (left, right)], axis=1
        )
        diag = bcast(sums[128 + SLOTS + 8 : 128 + SLOTS + 16, :], k) + 1.0
        high_half[8 + k] = jnp.where(sub == k, diag, corner)
    rhs = [sums[128:136, :], sums[136:144, :]]
    pivots = []
    values = []
    for k in range(SLOTS):
        halves = [low_half[k], high_half[k]] if k < 8 else [None, high_half[k]]
        inverse = 1.0 / bcast(halves[k // 8], k % 8)
        scaled = [None if h is None else h * inverse for h in halves]
        value = bcast(rhs[k // 8], k % 8)
        pivots.append(inverse)
        values.append(value)
        for h in range(2):
            if scaled[h] is not None:
                rhs[h] = rhs[h] - scaled[h] * value
        for j in range(k + 1, SLOTS):
            factor = bcast(scaled[j // 8], j % 8)
            if j < 8:
                low_half[j] = low_half[j] - factor * halves[0]
            high_half[j] = high_half[j] - factor * halves[1]
    x = [jnp.zeros((8, width), F32), jnp.zeros((8, width), F32)]
    for k in reversed(range(SLOTS)):
        acc = jnp.where(sub > k - 8, high_half[k] * x[1], 0.0)
        if k < 8:
            acc = acc + jnp.where(sub > k, low_half[k] * x[0], 0.0)
        solved = (values[k] - jnp.sum(acc, axis=0, keepdims=True)) * pivots[k]
        x[k // 8] = jnp.where(sub == k % 8, solved, x[k // 8])
    xs[0:8, :] = x[0]
    xs[8:16, :] = x[1]

    lane = iota((8, PW), 1)
    sub8 = iota((8, PW), 0)
    doubled = []
    for k in range(BANDS):
        tile = xs[:, PW * (k // 2) : PW * (k // 2 + 1)]
        turned = pltpu.roll(tile, 64, 1)
        wide = iota((SLOTS, PW), 1)
        doubled.append(
            jnp.where(wide < 64, tile, turned) if k % 2 == 0 else jnp.where(wide < 64, turned, tile)
        )
    pieces = []
    for n in range(8):
        piece = jnp.zeros((8, PW), F32)
        for k in range(BANDS):
            row = jnp.where(
                lane < 64,
                jnp.broadcast_to(doubled[k][2 * n : 2 * n + 1], (8, PW)),
                jnp.broadcast_to(doubled[k][2 * n + 1 : 2 * n + 2], (8, PW)),
            )
            piece = jnp.where(sub8 == k, row, piece)
        pieces.append(piece)
    flat = jnp.concatenate(pieces, axis=1)
    extent = SRC + 2 * EDGE
    slots = iota((SLOTS, BLOBS), 0)
    columns = jnp.transpose(jnp.where(slots < counts[...], members[...], -1).astype(F32))
    targets = iota((BLOBS, extent), 1)
    targets = jnp.where(targets < SRC, targets + EDGE, jnp.where(targets < SRC + EDGE, targets - SRC, targets))
    targets = targets.astype(F32)
    onehot = jnp.concatenate(
        [jnp.where(columns[:, j : j + 1] == targets, 1.0, 0.0).astype(BF16) for j in range(SLOTS)],
        axis=0,
    )
    fluxes = exact_left(flat, onehot, NN)
    own[...] = fluxes[:, 0:SRC]
    rim = fluxes[:, SRC:extent]
    before[...] = jnp.where(lane < EDGE, rim, 0.0)
    after[...] = jnp.where(lane < EDGE, 0.0, rim)


def edge_kernel(own, from_before, from_after, edge_rows, out):
    rim = pltpu.roll(from_before[...] + from_after[...], EDGE, 1)
    rows = edge_rows[...]
    targets = iota((2 * EDGE, SRC), 1)
    onehot = jnp.where(rows == targets, 1.0, 0.0).astype(BF16)
    out[...] = (own[...] + exact_left(rim, onehot, NN))[0:BANDS]


def call(kernel, out_shape, in_specs, scratch=(), out_specs=None):
    return pl.pallas_call(
        kernel,
        out_shape=out_shape,
        in_specs=in_specs,
        out_specs=VMEM if out_specs is None else out_specs,
        scratch_shapes=list(scratch),
        compiler_params=pltpu.CompilerParams(vmem_limit_bytes=48 * 1024 * 1024),
    )


def on_device(
    pixels,
    inv_var,
    tile_offset,
    psf_amp,
    psf_sigma,
    tile_blob,
    tile_band,
    source_pos,
    edge_rows,
    blob_members,
    sources_per_blob,
):
    zones = lax.axis_size("zone")
    bands = lax.axis_size("band")
    shape = jax.ShapeDtypeStruct
    counts = sources_per_blob.reshape(1, -1)
    members = jnp.transpose(blob_members)
    spread = call(table_kernel, shape((zones, TABLE_ROWS, PW), F32), [VMEM] * 4)(
        members, counts, source_pos, edge_rows.reshape(1, -1)
    )
    table = lax.all_to_all(spread, "zone", split_axis=0, concat_axis=0, tiled=True)
    tiles = pixels.shape[0]
    groups = tiles // GROUP
    steps = 4
    rows = pl.BlockSpec((tiles * PH // steps, PW), lambda n: (n, 0))
    roots, scaled = pl.pallas_call(
        prepare_kernel,
        grid=(steps,),
        out_shape=(
            shape((tiles * PH, PW), F32),
            shape((groups, PH // 2, 2 * GROUP, 2 * PW), BF16),
        ),
        in_specs=[rows, rows],
        out_specs=(
            rows,
            pl.BlockSpec((groups // steps, PH // 2, 2 * GROUP, 2 * PW), lambda n: (n, 0, 0, 0)),
        ),
        compiler_params=pltpu.CompilerParams(vmem_limit_bytes=48 * 1024 * 1024),
    )(pixels.reshape(tiles * PH, PW), inv_var.reshape(tiles * PH, PW))
    inverse = -LOG2E * (0.5 / (psf_sigma * psf_sigma))
    numbers = jnp.concatenate([tile_offset, psf_amp, inverse], axis=0)
    codes = (tile_blob * 4 + tile_band).reshape(1, -1)
    places, live_counts = call(
        place_kernel,
        (shape((groups, 2 * PW, PW), F32), shape((tiles, PW), F32)),
        [SMEM, VMEM],
        [
            pltpu.VMEM((zones, 8, PW), F32),
            pltpu.VMEM((tiles, PW), F32),
            pltpu.VMEM((tiles, 2 * PW), F32),
        ],
        (VMEM, VMEM),
    )(codes, table)
    terms = call(
        tile_kernel,
        shape((zones, 8, PW), F32),
        [SMEM] * 2 + [VMEM] * 4,
        [
            pltpu.VMEM((PH // 2, 2 * PW, 2 * PW), BF16),
            pltpu.VMEM((PH // 2, 2 * PW, 2 * PW), BF16),
            pltpu.SMEM((zones,), jnp.int32),
        ],
    )(codes, numbers, places, live_counts, roots, scaled)
    got = lax.all_to_all(terms, "zone", split_axis=0, concat_axis=0, tiled=True)
    systems = call(gather_kernel, shape((240, PW), F32), [VMEM])(got.reshape(zones * 8, PW))
    others = [
        lax.ppermute(systems, "band", [(i, (i + k) % bands) for i in range(bands)])
        for k in range(1, bands)
    ]
    own, before, after = call(
        solve_kernel,
        (shape((8, SRC), F32), shape((8, PW), F32), shape((8, PW), F32)),
        [VMEM] * 6,
        [pltpu.VMEM((160, PW), F32), pltpu.VMEM((160, PW), F32), pltpu.VMEM((SLOTS, 2 * PW), F32)],
        (VMEM, VMEM, VMEM),
    )(systems, *others, members, counts)
    up = [(i, i + 1) for i in range(zones - 1)]
    down = [(b, a) for a, b in up]
    from_before = lax.ppermute(after, "zone", up)
    from_after = lax.ppermute(before, "zone", down)
    return call(edge_kernel, shape((BANDS, SRC), F32), [VMEM] * 4)(
        own, from_before, from_after, edge_rows.reshape(-1, 1)
    )


def solution(mesh):
    tile = P(("zone", "band"))
    return jax.shard_map(
        on_device,
        mesh=mesh,
        in_specs=(
            P(("zone", "band"), None, None),
            P(("zone", "band"), None, None),
            P(None, ("zone", "band")),
            P(None, ("zone", "band")),
            P(None, ("zone", "band")),
            tile,
            tile,
            P(None, "zone"),
            P("zone"),
            P("zone", None),
            P("zone"),
        ),
        out_specs=P(None, "zone"),
        check_vma=False,
    )
```

```python
import functools

import jax
import jax.numpy as jnp
from jax import lax
from jax.experimental import pallas as pl
from jax.experimental.pallas import tpu as pltpu
from jax.sharding import PartitionSpec as P

BANDS = 3
SLOTS = 16
PH = 32
PW = 128
SRC = 512
BLOBS = 64
EDGE = 64
GROUP = 8
TABLE_ROWS = 16
MARK = 1000.0
LOG2E = 1.4426950408889634
F32 = jnp.float32
BF16 = jnp.bfloat16
NT = (((1,), (1,)), ((), ()))
NN = (((1,), (0,)), ((), ()))
TN = (((0,), (0,)), ((), ()))
VMEM = pl.BlockSpec(memory_space=pltpu.VMEM)
SMEM = pl.BlockSpec(memory_space=pltpu.SMEM)


def iota(shape, axis):
    return lax.broadcasted_iota(jnp.int32, shape, axis)


def three_parts(x):
    high = x.astype(BF16)
    rest = x - high.astype(F32)
    mid = rest.astype(BF16)
    low = (rest - mid.astype(F32)).astype(BF16)
    return high, mid, low


def dot(a, b, dims):
    return lax.dot_general(a, b, dims, preferred_element_type=F32)


def exact_left(x, onehot, dims):
    high, mid, low = three_parts(x)
    return (dot(low, onehot, dims) + dot(mid, onehot, dims)) + dot(high, onehot, dims)


def table_kernel(members, counts, source_pos, edge_rows, out):
    cnt = counts[...].astype(F32)
    above = iota((BLOBS, BLOBS), 0)
    beside = iota((BLOBS, BLOBS), 1)
    spread = jnp.broadcast_to(cnt, (BLOBS, BLOBS))
    start = jnp.sum(jnp.where(beside < above, spread, 0.0), axis=1, keepdims=True)
    own = jnp.sum(jnp.where(beside == above, spread, 0.0), axis=1, keepdims=True)
    start_row = jnp.sum(jnp.where(above == beside, start, 0.0), axis=0, keepdims=True)
    entry = iota((BLOBS, SRC), 1).astype(F32)
    inside = jnp.logical_and(entry >= start, entry < start + own)
    slot = jnp.sum(jnp.where(inside, entry - start, 0.0), axis=0, keepdims=True)
    picked = exact_left(members[...].astype(F32), inside.astype(BF16), NN)
    slot_ids = iota((SLOTS, SRC), 0).astype(F32)
    source = jnp.sum(jnp.where(slot_ids == slot, picked, 0.0), axis=0, keepdims=True)
    wanted = jnp.concatenate([source, edge_rows[...].astype(F32) + float(EDGE)], axis=1)
    width = SRC + 2 * EDGE
    row_ids = iota((SRC, width), 0).astype(F32) + float(EDGE)
    onehot = jnp.where(row_ids == wanted, 1.0, 0.0).astype(BF16)
    pos = jnp.concatenate([source_pos[...], jnp.zeros((6, SRC), F32)], axis=0)
    got = exact_left(pos, onehot, NN)
    lanes = iota((1, width), 1)
    mark = jnp.where(wanted < float(EDGE), wanted + (MARK + EDGE), wanted + (MARK - EDGE - SRC))
    outside = jnp.logical_or(wanted < float(EDGE), wanted >= float(EDGE + SRC))
    marked = jnp.logical_and(lanes < SRC, outside)
    got = jnp.where(marked, mark, got)
    rows = [got[p : p + 1, PW * n : PW * (n + 1)] for p in range(2) for n in range(4)]
    rows += [got[p : p + 1, SRC : SRC + PW] for p in range(2)]
    rows.append(jnp.concatenate([start_row, cnt], axis=1))
    rows.append(jnp.zeros((TABLE_ROWS - 11, PW), F32))
    table = jnp.concatenate(rows, axis=0)

    def write(z, _):
        out[z] = table
        return 0

    lax.fori_loop(0, out.shape[0], write, 0, unroll=8)


def prepare_kernel(pixels, weights, roots, scaled):
    def group(g, _):
        base = pl.multiple_of(g * (GROUP * PH), GROUP * PH)
        for i in range(PH):
            root = jnp.sqrt(weights[pl.ds(base + i, GROUP, stride=PH), :])
            roots[pl.ds(base + GROUP * i, GROUP), :] = root
            product = root * pixels[pl.ds(base + i, GROUP, stride=PH), :]
            high = product.astype(BF16).astype(F32)
            both = jnp.concatenate([high, product - high], axis=0)
            scaled[g, i // 2, :, PW * (i % 2) : PW * (i % 2 + 1)] = both.astype(BF16)
        return 0

    lax.fori_loop(0, scaled.shape[0], group, 0)


def place_kernel(code_s, table, places, counts, full, info, ranges):
    zones = table.shape[0]
    tiles = info.shape[0]
    lane = iota((8, PW), 1)
    sub = iota((8, PW), 0)
    lane16 = iota((SLOTS, PW), 1).astype(F32)
    slot_f = iota((SLOTS, PW), 0).astype(F32)

    def patch(z, _):
        before = jnp.maximum(z - 1, 0)
        after = jnp.minimum(z + 1, zones - 1)
        value = table[z, 0:8, :]
        sides = []
        for row in (8, 9):
            low = jnp.broadcast_to(table[before, row : row + 1, :], (8, PW))
            high = jnp.broadcast_to(table[after, row : row + 1, :], (8, PW))
            sides.append(jnp.where(lane < EDGE, high, low))
        edges = jnp.where(sub < 4, sides[0], sides[1])
        at = jnp.clip(value.astype(jnp.int32) - int(MARK), 0, PW - 1)
        found = jnp.take_along_axis(edges, at, axis=1, mode="promise_in_bounds")
        full[z] = jnp.where(value >= MARK, found, value)
        return 0

    lax.fori_loop(0, zones, patch, 0, unroll=16)

    def pick(t, _):
        blob = code_s[0, t] >> 2
        row = table[blob >> 6, 10:11, :]
        info[pl.ds(t, 1), :] = jnp.where((lane[0:1] & (BLOBS - 1)) == (blob & (BLOBS - 1)), row, 0.0)
        return 0

    lax.fori_loop(0, tiles, pick, 0, unroll=32)
    half = iota((PW, 2 * PW), 0) // BLOBS == iota((PW, 2 * PW), 1) // PW
    ranges[...] = exact_left(info[...], jnp.where(half, 1.0, 0.0).astype(BF16), NN)
    counts[...] = ranges[:, PW : 2 * PW]
    ones = jnp.ones((3 * PW, PW), BF16)

    def positions(g, _):
        picked = [[], []]
        spans = ranges[pl.ds(pl.multiple_of(g * GROUP, GROUP), GROUP), :]
        for s in range(GROUP):
            t = g * GROUP + s
            zone = code_s[0, t] >> 8
            start = jnp.broadcast_to(spans[s : s + 1, 0:PW], (SLOTS, PW))
            index = start + slot_f
            hits = [index == lane16 + float(PW * n) for n in range(4)]
            for p in range(2):
                value = jnp.zeros((SLOTS, PW), F32)
                for n in range(4):
                    row = full[zone, 4 * p + n : 4 * p + n + 1, :]
                    value = jnp.where(hits[n], jnp.broadcast_to(row, (SLOTS, PW)), value)
                picked[p].append(value)
        parts = three_parts(jnp.concatenate(picked[0] + picked[1], axis=0))
        places[g] = dot(jnp.concatenate(parts, axis=1), ones, NN)
        return 0

    lax.fori_loop(0, tiles // GROUP, positions, 0, unroll=4)


def tile_kernel(
    code_s,
    par_s,
    places,
    counts,
    roots,
    scaled,
    out,
    buf_a,
    buf_b,
    used,
):
    zones = out.shape[0]
    tiles = counts.shape[0]
    lane = iota((8, PW), 1)
    sub = iota((8, PW), 0)
    lane16 = iota((SLOTS, PW), 1).astype(F32)
    slot_f = iota((SLOTS, PW), 0).astype(F32)
    spot = lane >> 4
    entry = lane & (SLOTS - 1)

    def clear(z, _):
        out[z] = jnp.zeros((8, PW), F32)
        used[z] = 0
        return 0

    lax.fori_loop(0, zones, clear, 0)

    def store(g, buf, s, i, total):
        root = roots[pl.ds(GROUP * (PH * g + i) + s, 1), :]
        total = total * jnp.broadcast_to(root, (SLOTS, PW))
        high = total.astype(BF16)
        low = (total - high.astype(F32)).astype(BF16)
        first = pl.multiple_of(SLOTS * s, SLOTS)
        side = slice(PW * (i % 2), PW * (i % 2 + 1))
        buf[i // 2, pl.ds(first, SLOTS), side] = low
        buf[i // 2, pl.ds(128 + first, SLOTS), side] = high

    def render(g, s, buf, meanwhile):
        t = g * GROUP + s
        first = pl.multiple_of(SLOTS * s, SLOTS)
        y = places[g, pl.ds(first, SLOTS), :]
        x = places[g, pl.ds(128 + first, SLOTS), :]
        count = jnp.broadcast_to(counts[pl.ds(t, 1), :], (SLOTS, PW))
        live = jnp.where(slot_f < count, 1.0, 0.0)
        dx = (lane16 - par_s[1, t]) - x
        dx = dx * dx
        dy = (float(PH // 2) - par_s[0, t]) - y
        flat = jnp.zeros((8, PW), F32)
        here, up, down, turn = [], [], [], []
        for c in range(3):
            scale = par_s[5 + c, t]
            col = jnp.exp2(scale * dx) * (live * par_s[2 + c, t])
            here.append(jnp.exp2(scale * (dy * dy)) * col)
            up.append(jnp.exp2(scale * (2.0 * dy + 1.0)))
            down.append(jnp.exp2(scale * (1.0 - 2.0 * dy)))
            step = jnp.exp2(flat + 2.0 * scale)
            turn.append(jnp.concatenate([step, step], axis=0))
        store(g, buf, s, PH // 2, (here[0] + here[1]) + here[2])
        above, below = list(here), list(here)
        for n in range(1, PH // 2 + 1):
            if n in meanwhile:
                meanwhile[n]()
            for c in range(3):
                below[c] = below[c] * down[c]
                down[c] = down[c] * turn[c]
            store(g, buf, s, PH // 2 - n, (below[0] + below[1]) + below[2])
            if n < PH // 2:
                for c in range(3):
                    above[c] = above[c] * up[c]
                    up[c] = up[c] * turn[c]
                store(g, buf, s, PH // 2 + n, (above[0] + above[1]) + above[2])

    def finish(g, prod, sides):
        cross = prod[0:128, 0:128]
        gram = prod[0:128, 128:256] + (cross + jnp.transpose(cross))
        rhs8 = sides[0:8, 128:256] + (sides[0:8, 0:128] + sides[8:16, 128:256])
        upper = jnp.zeros((8, PW), F32)
        lower = jnp.zeros((8, PW), F32)
        for s in range(GROUP):
            upper = jnp.where(spot == s, gram[SLOTS * s : SLOTS * s + 8], upper)
            lower = jnp.where(spot == s, gram[SLOTS * s + 8 : SLOTS * s + 16], lower)
        fold = jnp.where(entry < sub, pltpu.roll(lower, PW - 8, 1), upper)
        diag = jnp.sum(jnp.where(entry == sub + 8, lower, 0.0), axis=0, keepdims=True)
        rhs = jnp.sum(jnp.where(spot == sub, rhs8, 0.0), axis=0, keepdims=True)
        label = jnp.zeros((1, PW), F32)
        for s in range(GROUP):
            t = g * GROUP + s
            code = (code_s[0, t] & 3) * BLOBS + ((code_s[0, t] >> 2) & (BLOBS - 1)) + 1
            label = jnp.where(lane[0:1] == SLOTS * s, code.astype(F32), label)
        extra = jnp.where(sub == 0, rhs, jnp.where(sub == 1, diag + label, 0.0))
        for s in range(GROUP):
            t = g * GROUP + s
            zone = code_s[0, t] >> 8
            place = used[zone]
            used[zone] = place + 1
            shift = SLOTS * (place - s)
            value = jnp.where(
                lane < 64,
                pltpu.roll(fold, (shift + 128) & 127, 1),
                pltpu.roll(extra, (shift + 192) & 127, 1),
            )
            mine = (spot & 3) == place
            out[zone] = jnp.where(mine, value, out[zone])

    def run(sum_a, sum_b, rhs_a, rhs_b):
        def load(buf, k, unit, stage):
            pltpu.matmul_push_rhs(buf[k, 0:256, :], stage, unit, transpose=True)

        def multiply(g, buf, k, unit, stage):
            pltpu.matmul_acc_lhs((sum_a, sum_b)[unit], buf[k, 128:256, :], load_staged_rhs=stage)
            pltpu.matmul_acc_lhs((rhs_a, rhs_b)[unit], scaled[g, k])

        def total():
            gram = pltpu.matmul_pop(sum_a) + pltpu.matmul_pop(sum_b)
            return gram, pltpu.matmul_pop(rhs_a) + pltpu.matmul_pop(rhs_b)

        def both(g, buf, before, done):

            def pair(u, _):
                steps = [{}, {}]
                if before is not None:
                    for stage in range(2):
                        for unit in range(2):
                            work = (4 * u + 2 * stage + unit, unit, stage)
                            n = 2 * (2 * stage + unit) + 1
                            steps[0][n] = functools.partial(load, before[1], *work)
                            n = 8 * (1 - stage) + 2 * unit + 1
                            steps[stage][n] = functools.partial(multiply, *before, *work)
                for half in range(2):
                    render(g, 2 * u + half, buf, steps[half])
                return 0

            if done is not None:
                finish(done, *total())
            pair(jnp.int32(0), 0)
            lax.fori_loop(1, GROUP // 2, pair, 0)

        def last(g, buf):
            for k in range(2 * GROUP):
                load(buf, k, k % 2, k // 2 % 2)
                multiply(g, buf, k, k % 2, k // 2 % 2)
            finish(g, *total())

        groups = tiles // GROUP
        both(0, buf_a, None, None)
        both(1, buf_b, (0, buf_a), None)

        def step(n, _):
            both(2 * n, buf_a, (2 * n - 1, buf_b), 2 * n - 2)
            both(2 * n + 1, buf_b, (2 * n, buf_a), 2 * n - 1)
            return 0

        lax.fori_loop(1, groups // 2, step, 0)
        finish(groups - 2, *total())
        last(groups - 1, buf_b)

    shapes = [pltpu.ACC(unit)((rows, 256), F32) for rows in (128, 16) for unit in range(2)]
    pl.run_scoped(run, *shapes)


def gather_kernel(got, out):
    zones = got.shape[0] // 8
    lane = iota((zones, PW), 1)
    spot = lane >> 4
    parts = [got[pl.ds(r, zones, stride=8), :] for r in range(8)]
    body = []
    for s in range(4):
        main = jnp.zeros((zones, PW), F32)
        for r in range(8):
            shift = (SLOTS * (r - s)) % PW
            moved = pltpu.roll(parts[r], shift, 1) if shift else parts[r]
            main = jnp.where(spot == r, moved, main)
        rhs = pltpu.roll(parts[0], (64 - SLOTS * s) % PW, 1)
        rest = pltpu.roll(parts[1], (64 + SLOTS - SLOTS * s) % PW, 1)
        extra = jnp.where(spot == 0, rhs, jnp.where(spot == 1, rest, 0.0))
        body.append(jnp.concatenate([main, extra], axis=1))
    values = jnp.concatenate(body, axis=0)
    label = values[:, PW + SLOTS : PW + SLOTS + 1]
    systems = 2 * PW
    codes = iota((4 * zones, systems), 1).astype(F32) + 1.0
    onehot = jnp.where(label == codes, 1.0, 0.0).astype(BF16)
    total = exact_left(values, onehot, TN)
    out[0:160] = total[0:160, 0:PW]
    turned = pltpu.roll(total[80:160, PW:systems], EDGE, 1)
    out[160:240] = jnp.where(iota((80, PW), 1) < EDGE, total[0:80, PW:systems], turned)


def solve_kernel(first, second, third, fourth, members, counts, own, before, after, left, right, xs):
    both = (first[...] + second[...]) + (third[...] + fourth[...])
    width = 2 * PW
    left[...] = both[0:160]
    right[0:80] = both[160:240]
    right[80:160] = pltpu.roll(both[160:240], EDGE, 1)
    sums = jnp.concatenate([left[...], right[...]], axis=1)
    sub = iota((8, width), 0)

    def bcast(x, k):
        return jnp.broadcast_to(x[k : k + 1], (8, width))

    low_half = [None] * SLOTS
    high_half = [None] * SLOTS
    for k in range(8):
        low_half[k] = sums[SLOTS * k : SLOTS * k + 8, :] + jnp.where(sub == k, 1.0, 0.0)
        high_half[k] = sums[SLOTS * k + 8 : SLOTS * k + 16, :]
        corner = jnp.concatenate(
            [half[pl.ds(k, 8, stride=SLOTS), :] for half in (left, right)], axis=1
        )
        diag = bcast(sums[128 + SLOTS + 8 : 128 + SLOTS + 16, :], k) + 1.0
        high_half[8 + k] = jnp.where(sub == k, diag, corner)
    rhs = [sums[128:136, :], sums[136:144, :]]
    pivots = []
    values = []
    for k in range(SLOTS):
        halves = [low_half[k], high_half[k]] if k < 8 else [None, high_half[k]]
        inverse = 1.0 / bcast(halves[k // 8], k % 8)
        scaled = [None if h is None else h * inverse for h in halves]
        value = bcast(rhs[k // 8], k % 8)
        pivots.append(inverse)
        values.append(value)
        for h in range(2):
            if scaled[h] is not None:
                rhs[h] = rhs[h] - scaled[h] * value
        for j in range(k + 1, SLOTS):
            factor = bcast(scaled[j // 8], j % 8)
            if j < 8:
                low_half[j] = low_half[j] - factor * halves[0]
            high_half[j] = high_half[j] - factor * halves[1]
    x = [jnp.zeros((8, width), F32), jnp.zeros((8, width), F32)]
    for k in reversed(range(SLOTS)):
        acc = jnp.where(sub > k - 8, high_half[k] * x[1], 0.0)
        if k < 8:
            acc = acc + jnp.where(sub > k, low_half[k] * x[0], 0.0)
        solved = (values[k] - jnp.sum(acc, axis=0, keepdims=True)) * pivots[k]
        x[k // 8] = jnp.where(sub == k % 8, solved, x[k // 8])
    xs[0:8, :] = x[0]
    xs[8:16, :] = x[1]

    lane = iota((8, PW), 1)
    sub8 = iota((8, PW), 0)
    doubled = []
    for k in range(BANDS):
        tile = xs[:, PW * (k // 2) : PW * (k // 2 + 1)]
        turned = pltpu.roll(tile, 64, 1)
        wide = iota((SLOTS, PW), 1)
        doubled.append(
            jnp.where(wide < 64, tile, turned) if k % 2 == 0 else jnp.where(wide < 64, turned, tile)
        )
    pieces = []
    for n in range(8):
        piece = jnp.zeros((8, PW), F32)
        for k in range(BANDS):
            row = jnp.where(
                lane < 64,
                jnp.broadcast_to(doubled[k][2 * n : 2 * n + 1], (8, PW)),
                jnp.broadcast_to(doubled[k][2 * n + 1 : 2 * n + 2], (8, PW)),
            )
            piece = jnp.where(sub8 == k, row, piece)
        pieces.append(piece)
    flat = jnp.concatenate(pieces, axis=1)
    extent = SRC + 2 * EDGE
    slots = iota((SLOTS, BLOBS), 0)
    columns = jnp.transpose(jnp.where(slots < counts[...], members[...], -1).astype(F32))
    targets = iota((BLOBS, extent), 1)
    targets = jnp.where(targets < SRC, targets + EDGE, jnp.where(targets < SRC + EDGE, targets - SRC, targets))
    targets = targets.astype(F32)
    onehot = jnp.concatenate(
        [jnp.where(columns[:, j : j + 1] == targets, 1.0, 0.0).astype(BF16) for j in range(SLOTS)],
        axis=0,
    )
    fluxes = exact_left(flat, onehot, NN)
    own[...] = fluxes[:, 0:SRC]
    rim = fluxes[:, SRC:extent]
    before[...] = jnp.where(lane < EDGE, rim, 0.0)
    after[...] = jnp.where(lane < EDGE, 0.0, rim)


def edge_kernel(own, from_before, from_after, edge_rows, out):
    rim = pltpu.roll(from_before[...] + from_after[...], EDGE, 1)
    rows = edge_rows[...]
    targets = iota((2 * EDGE, SRC), 1)
    onehot = jnp.where(rows == targets, 1.0, 0.0).astype(BF16)
    out[...] = (own[...] + exact_left(rim, onehot, NN))[0:BANDS]


def call(kernel, out_shape, in_specs, scratch=(), out_specs=None):
    return pl.pallas_call(
        kernel,
        out_shape=out_shape,
        in_specs=in_specs,
        out_specs=VMEM if out_specs is None else out_specs,
        scratch_shapes=list(scratch),
        compiler_params=pltpu.CompilerParams(vmem_limit_bytes=48 * 1024 * 1024),
    )


def on_device(
    pixels,
    inv_var,
    tile_offset,
    psf_amp,
    psf_sigma,
    tile_blob,
    tile_band,
    source_pos,
    edge_rows,
    blob_members,
    sources_per_blob,
):
    zones = lax.axis_size("zone")
    bands = lax.axis_size("band")
    shape = jax.ShapeDtypeStruct
    counts = sources_per_blob.reshape(1, -1)
    members = jnp.transpose(blob_members)
    spread = call(table_kernel, shape((zones, TABLE_ROWS, PW), F32), [VMEM] * 4)(
        members, counts, source_pos, edge_rows.reshape(1, -1)
    )
    table = lax.all_to_all(spread, "zone", split_axis=0, concat_axis=0, tiled=True)
    tiles = pixels.shape[0]
    groups = tiles // GROUP
    steps = 4
    rows = pl.BlockSpec((tiles * PH // steps, PW), lambda n: (n, 0))
    roots, scaled = pl.pallas_call(
        prepare_kernel,
        grid=(steps,),
        out_shape=(
            shape((tiles * PH, PW), F32),
            shape((groups, PH // 2, 2 * GROUP, 2 * PW), BF16),
        ),
        in_specs=[rows, rows],
        out_specs=(
            rows,
            pl.BlockSpec((groups // steps, PH // 2, 2 * GROUP, 2 * PW), lambda n: (n, 0, 0, 0)),
        ),
        compiler_params=pltpu.CompilerParams(vmem_limit_bytes=48 * 1024 * 1024),
    )(pixels.reshape(tiles * PH, PW), inv_var.reshape(tiles * PH, PW))
    inverse = -LOG2E * (0.5 / (psf_sigma * psf_sigma))
    numbers = jnp.concatenate([tile_offset, psf_amp, inverse], axis=0)
    codes = (tile_blob * 4 + tile_band).reshape(1, -1)
    places, live_counts = call(
        place_kernel,
        (shape((groups, 2 * PW, PW), F32), shape((tiles, PW), F32)),
        [SMEM, VMEM],
        [
            pltpu.VMEM((zones, 8, PW), F32),
            pltpu.VMEM((tiles, PW), F32),
            pltpu.VMEM((tiles, 2 * PW), F32),
        ],
        (VMEM, VMEM),
    )(codes, table)
    terms = call(
        tile_kernel,
        shape((zones, 8, PW), F32),
        [SMEM] * 2 + [VMEM] * 4,
        [
            pltpu.VMEM((PH // 2, 2 * PW, 2 * PW), BF16),
            pltpu.VMEM((PH // 2, 2 * PW, 2 * PW), BF16),
            pltpu.SMEM((zones,), jnp.int32),
        ],
    )(codes, numbers, places, live_counts, roots, scaled)
    got = lax.all_to_all(terms, "zone", split_axis=0, concat_axis=0, tiled=True)
    systems = call(gather_kernel, shape((240, PW), F32), [VMEM])(got.reshape(zones * 8, PW))
    others = [
        lax.ppermute(systems, "band", [(i, (i + k) % bands) for i in range(bands)])
        for k in range(1, bands)
    ]
    own, before, after = call(
        solve_kernel,
        (shape((8, SRC), F32), shape((8, PW), F32), shape((8, PW), F32)),
        [VMEM] * 6,
        [pltpu.VMEM((160, PW), F32), pltpu.VMEM((160, PW), F32), pltpu.VMEM((SLOTS, 2 * PW), F32)],
        (VMEM, VMEM, VMEM),
    )(systems, *others, members, counts)
    up = [(i, i + 1) for i in range(zones - 1)]
    down = [(b, a) for a, b in up]
    from_before = lax.ppermute(after, "zone", up)
    from_after = lax.ppermute(before, "zone", down)
    return call(edge_kernel, shape((BANDS, SRC), F32), [VMEM] * 4)(
        own, from_before, from_after, edge_rows.reshape(-1, 1)
    )


def solution(mesh):
    tile = P(("zone", "band"))
    return jax.shard_map(
        on_device,
        mesh=mesh,
        in_specs=(
            P(("zone", "band"), None, None),
            P(("zone", "band"), None, None),
            P(None, ("zone", "band")),
            P(None, ("zone", "band")),
            P(None, ("zone", "band")),
            tile,
            tile,
            P(None, "zone"),
            P("zone"),
            P("zone", None),
            P("zone"),
        ),
        out_specs=P(None, "zone"),
        check_vma=False,
    )
```
